256 devices in a mesh: tm: 8 (over y, core), sub: 32 (over x, z).
Axes of the slice: x: 4, y: 4, z: 8, core: 2. Of those that a mesh axis runs over, the one named last changes fastest.
Arguments:
- flex: bfloat16 [32, 2048, 2048], P('sub'), as said below
- mass: float32 [32, 2048], P('sub'), may hold values from 0.25 to 1
- coarse_rate: float32 [32, 2048], P('sub'), may hold values from 0.05 to 1
- face_perm: int32 [32, 1024], P('sub'), may hold values from 0 to 1023, each once within a row
- start_u: float32 [8, 32, 2048, 128], P('tm', 'sub'), may hold values from -6 to 6
- start_v: float32 [8, 32, 2048, 128], P('tm', 'sub'), may hold values from -6 to 6
- load: bfloat16 [8, 32, 2048, 128], P('tm', 'sub'), may hold values from -16 to 16
Outputs:
- end_u: float32 [8, 32, 2048, 128], P('tm', 'sub')
- end_v: float32 [8, 32, 2048, 128], P('tm', 'sub')
The draws below stay inside these ranges and needn't reach their ends.
Inputs may be any that keep to these rules, and one draw needn't show every extreme that they name: Every row of face_perm holds each of 0 to 1023 once. flex[s] is symmetric positive definite, entries within -0.5 to 0.5.
All inputs are finite; a program needn't handle non-finite values.
Results may differ from the reference program's by a relative error of at most 0.0019.
Values sent between devices are 32-bit elements; how exact they have to be, the bound alone decides.
No kernel may reach another device: no remote copies, remote signals or barrier semaphores. Data moves between devices by JAX's collectives and lax.ppermute only.
A program may use at most 128 MiB of HBM per device.

```python
import math
import jax
import jax.numpy as jnp
from jax import lax

FACE = 1024
IFACE = 2048
R = 128
FINE = 2
DUAL = 2
SLICES = 8
SUBS = 32


def draw_flex(key, part):
    key = jax.random.fold_in(key, 11)
    key_diag, key_gain, key_noise = jax.random.split(key, 3)
    diag = jax.random.uniform(key_diag, (SUBS, IFACE), jnp.float32, 0.5, 1.5)
    gain = jax.random.uniform(key_gain, (SUBS, IFACE), jnp.float32, 0.4, 1.0)
    noise = jax.random.uniform(key_noise, (SUBS, IFACE, IFACE), jnp.float32, -1.0, 1.0)
    noise = 0.5 * (noise + jnp.swapaxes(noise, 1, 2)) * (0.15 * IFACE ** (-0.5))
    reach = IFACE / 8.0
    place = jnp.arange(IFACE).astype(jnp.float32)
    kernel = 4.0 / reach * jnp.exp(-jnp.abs(place[:, None] - place[None, :]) / reach)
    ident = jnp.eye(IFACE, dtype=jnp.float32)
    whole = diag[:, :, None] * ident[None] + gain[:, :, None] * gain[:, None, :] * kernel[None] + noise
    return (0.04 * whole).astype(jnp.bfloat16)


def shard_levels(key, shape, pieces, least, largest):
    loudness, own = 1.0, jax.random.fold_in(key, 6)
    for position, shards_of in pieces:
        draws = jnp.exp(jax.random.uniform(jax.random.fold_in(own, position), (shards_of,), jnp.float32, least / len(pieces), largest / len(pieces)))
        loudness = loudness * jnp.repeat(draws, shape[position] // shards_of).reshape([-1 if axis == position else 1 for axis in range(len(shape))])
    return loudness


def centred(stream_key, dims, scale, limit, cuts=(), held_as=jnp.bfloat16):
    level = shard_levels(stream_key, dims, cuts, -0.22, 0.18) if cuts else 1.0
    values = jax.random.normal(stream_key, dims, jnp.float32) * scale * level
    return jnp.minimum(jnp.maximum(values, -limit), limit).astype(held_as)


def setup_inputs(seed: int = 0) -> dict:
    splits = jax.random.split(jax.random.key(seed), 8)
    flex = draw_flex(jax.random.fold_in(splits[7], 71), 0)
    mass = jnp.clip(jnp.exp(math.log(1.0) - 1.3862944 * jax.random.uniform(splits[1], (SUBS, IFACE), jnp.float32) ** shard_levels(splits[1], (SUBS, IFACE), ((0, 32),), -0.2, 0.2)), 0.25, 1.0)
    coarse_rate = jnp.clip(jnp.exp(math.log(1.0) - 2.9957323 * jax.random.uniform(splits[2], (SUBS, IFACE), jnp.float32) ** shard_levels(splits[2], (SUBS, IFACE), ((0, 32),), -0.2, 0.2)), 0.05, 1.0)
    face_perm = jax.vmap(lambda own: jax.random.permutation(own, FACE))(jax.random.split(splits[3], SUBS)).reshape((SUBS, FACE)).astype(jnp.int32)
    start_u = centred(splits[4], (SLICES, SUBS, IFACE, R), 1.0, 6.0, ((0, 8), (1, 32)), jnp.float32)
    start_v = centred(splits[5], (SLICES, SUBS, IFACE, R), 1.0, 6.0, ((0, 8), (1, 32)), jnp.float32)
    load = centred(splits[6], (SLICES, SUBS, IFACE, R), 4.0, 16.0, ((0, 8), (1, 32)))
    return dict(flex=flex, mass=mass, coarse_rate=coarse_rate, face_perm=face_perm, start_u=start_u, start_v=start_v, load=load)


def apply_all(flex32, z):
    zb = lax.optimization_barrier(z.astype(jnp.bfloat16)).astype(jnp.float32)
    return jnp.einsum("sij,sjr->sir", flex32, zb)


def lift_all(p, face_perm):
    prior = jnp.concatenate([jnp.zeros_like(p[:1]), p[:-1]], axis=0)
    left = -jax.vmap(lambda block, perm: jnp.take(block, perm, axis=0))(prior, face_perm)
    return jnp.concatenate([left, p], axis=1)


def gap_all(y, face_perm):
    left = y[:, :FACE]
    scattered = jax.vmap(lambda block, perm: jnp.zeros_like(block).at[perm].set(block))(left, face_perm)
    after = jnp.concatenate([scattered[1:], jnp.zeros_like(scattered[:1])], axis=0)
    gap = y[:, FACE:] - after
    keep = (jnp.arange(SUBS) < SUBS - 1)[:, None, None]
    return jnp.where(keep, gap, jnp.zeros_like(gap))


def inner(a, b):
    return jnp.sum(a * b, axis=(0, 1))


def propagate(flex32, mass, face_perm, u, v, force):
    for step in range(FINE):
        pred = u + v
        rhs = force + 2.0 * mass[:, :, None] * pred
        y = apply_all(flex32, rhs)
        res = gap_all(y, face_perm)
        p = res
        rr = inner(res, res)
        accum = jnp.zeros_like(y)
        for k in range(DUAL):
            q = apply_all(flex32, lift_all(p, face_perm))
            w = gap_all(q, face_perm)
            alpha = rr / inner(p, w)
            accum = accum + alpha[None, None, :] * q
            if k + 1 < DUAL:
                res = res - alpha[None, None, :] * w
                fresh = inner(res, res)
                p = res + (fresh / rr)[None, None, :] * p
                rr = fresh
        u_new = y - accum
        v = v + 2.0 * (u_new - pred)
        u = u_new
    return u, v


def reference(flex, mass, coarse_rate, face_perm, start_u, start_v, load):
    flex32 = flex.astype(jnp.float32)

    def one_slice(items):
        u, v, force = items
        return propagate(flex32, mass, face_perm, u, v, force.astype(jnp.float32))

    fine_u, fine_v = lax.map(one_slice, (start_u, start_v, load))
    rate = coarse_rate[:, :, None]
    span = float(FINE)
    denom = 1.0 + rate
    outs_u = [fine_u[0]]
    outs_v = [fine_v[0]]
    for t in range(1, SLICES):
        du = outs_u[-1] - start_u[t]
        dv = outs_v[-1] - start_v[t]
        gu = ((1.0 - rate) * du + span * dv) / denom
        gv = (-(4.0 * rate / span) * du + (1.0 - rate) * dv) / denom
        outs_u.append(fine_u[t] + gu)
        outs_v.append(fine_v[t] + gv)
    return jnp.stack(outs_u, axis=0), jnp.stack(outs_v, axis=0)
```

```python
import functools

import jax
import jax.numpy as jnp
from jax import lax
from jax.experimental import pallas as pl
from jax.experimental.pallas import tpu as pltpu
from jax.sharding import PartitionSpec as P

F32 = jnp.float32
BF16 = jnp.bfloat16
VMEM = pl.BlockSpec(memory_space=pltpu.VMEM)


def call(kernel, name, outs, args, flops=0):
    moved = sum(a.size * a.dtype.itemsize for a in args)
    return pl.pallas_call(
        kernel,
        name=name,
        out_shape=[jax.ShapeDtypeStruct(shape, dtype) for shape, dtype in outs],
        in_specs=[VMEM] * len(args),
        out_specs=[VMEM] * len(outs),
        compiler_params=pltpu.CompilerParams(vmem_limit_bytes=44 * 2**20),
        cost_estimate=pl.CostEstimate(flops=flops, bytes_accessed=moved, transcendentals=0),
    )(*args)


def pair(value):
    high = value.astype(BF16)
    return high, (value - high.astype(F32)).astype(BF16)


def triple(value):
    high = value.astype(BF16)
    rest = value - high.astype(F32)
    middle = rest.astype(BF16)
    low = (rest - middle.astype(F32)).astype(BF16)
    return jnp.concatenate([high, middle, low], axis=1)


def fold(wide):
    return wide[:, :128] + wide[:, 128:256] + wide[:, 256:]


def to_multipliers(onehot, face):
    return fold(jnp.dot(onehot, triple(face), preferred_element_type=F32))


def to_left(onehot, block):
    return fold(lax.dot_general(onehot, triple(block), (((0,), (0,)), ((), ())), preferred_element_type=F32))


def column(row):
    width = row.shape[1]
    return jnp.concatenate([jnp.transpose(jnp.broadcast_to(row[:, k : k + 128], (128, 128))) for k in range(0, width, 128)], axis=0)


def split_faces(field, left_ref, right_ref):
    half = left_ref.shape[0]
    left_ref[...] = field[:half]
    right_ref[...] = field[half:]


def start_kernel(a, u, v, load, mass, perm, y_l, y_r, y_m, onehot):
    width = perm.shape[1]
    onehot[...] = (lax.broadcasted_iota(jnp.int32, (width, width), 0) == perm[...]).astype(F32).astype(BF16)
    rhs = load[...].astype(F32) + 2.0 * column(mass[...]) * (u[...] + v[...])
    y = jnp.dot(a[...], rhs.astype(BF16), preferred_element_type=F32)
    split_faces(y, y_l, y_r)
    y_m[...] = to_multipliers(onehot[...], y_l[...])


def jump(onehot, f_l, f_r, from_left, from_right):
    sub = lax.axis_index("sub")
    left = jnp.where(sub == 0, 0.0, f_l[...] - to_left(onehot[...], from_left[...]))
    right = jnp.where(sub == lax.axis_size("sub") - 1, 0.0, f_r[...] - from_right[...])
    return left, right


def apply_wide(a, left, right):
    high_l, low_l = pair(left)
    high_r, low_r = pair(right)
    z = jnp.concatenate([jnp.concatenate([high_l, low_l], axis=1), jnp.concatenate([high_r, low_r], axis=1)], axis=0)
    return jnp.dot(a[...], z, preferred_element_type=F32)


def add_up(value):
    return jnp.sum(value, axis=0, keepdims=True)


def first_kernel(a, onehot, y_l, y_r, from_left, from_right, q_l, q_r, q_m, t_l, t_r, sums):
    half = y_l.shape[0]
    left, right = jump(onehot, y_l, y_r, from_left, from_right)
    wide = apply_wide(a, left, right)
    q = wide[:, :128]
    split_faces(q, q_l, q_r)
    q_m[...] = to_multipliers(onehot[...], q_l[...])
    split_faces(q + wide[:, 128:], t_l, t_r)
    rr = add_up(right * right)
    pw = add_up(left * q[:half]) + add_up(right * q[half:])
    sums[...] = jnp.concatenate([rr, pw, jnp.zeros((6, 128), F32)], axis=0)


def second_kernel(a, onehot, q_l, q_r, from_left, from_right, sums, s_l, s_r, spread):
    half = q_l.shape[0]
    left, right = jump(onehot, q_l, q_r, from_left, from_right)
    wide = apply_wide(a, left, right)
    s = wide[:, :128] + wide[:, 128:]
    split_faces(s, s_l, s_r)
    ww = add_up(right * right)
    wfw = add_up(left * s[:half]) + add_up(right * s[half:])
    own = jnp.concatenate([sums[:2], ww, wfw, jnp.zeros((4, 128), F32)], axis=0)
    spread[...] = jnp.broadcast_to(own[None], spread.shape)


def corrected(gathered, y_l, y_r, q_l, q_r, t_l, t_r, s_l, s_r):
    total = jnp.sum(gathered[...], axis=0)
    rr, pw, ww, wfw = total[0:1], total[1:2], total[2:3], total[3:4]
    alpha = rr / pw
    ratio = ww / pw
    later = (alpha * alpha * ww - rr) / (alpha * alpha * (wfw - ww * ratio))
    gain = alpha * later

    def face(y, q, t, s):
        return y[...] - alpha * q[...] - gain * (ratio * t[...] - s[...])

    return jnp.concatenate([face(y_l, q_l, t_l, s_l), face(y_r, q_r, t_r, s_r)], axis=0)


def next_kernel(a, onehot, gathered, y_l, y_r, q_l, q_r, t_l, t_r, s_l, s_r, u, v, load, mass, z_l, z_r, z_m, held):
    u_new = corrected(gathered, y_l, y_r, q_l, q_r, t_l, t_r, s_l, s_r)
    v_new = v[...] + 2.0 * (u_new - (u[...] + v[...]))
    pred = u_new + v_new
    rhs = load[...].astype(F32) + 2.0 * column(mass[...]) * pred
    y = jnp.dot(a[...], rhs.astype(BF16), preferred_element_type=F32)
    split_faces(y, z_l, z_r)
    z_m[...] = to_multipliers(onehot[...], z_l[...])
    held[...] = v_new - 2.0 * pred


def coarse(rate):
    scale = 1.0 / (1.0 + rate)
    return (1.0 - rate) * scale, 2.0 * scale, -2.0 * rate * scale


def finish_kernel(gathered, y_l, y_r, q_l, q_r, t_l, t_r, s_l, s_r, u, v, held, rate, out):
    u_new = corrected(gathered, y_l, y_r, q_l, q_r, t_l, t_r, s_l, s_r)
    v_new = held[...] + 2.0 * u_new
    same, up, down = coarse(column(rate[...]))
    keep = lax.axis_index("tm") == 0
    own_u = u_new - jnp.where(keep, 0.0, same * u[...] + up * v[...])
    own_v = v_new - jnp.where(keep, 0.0, down * u[...] + same * v[...])
    parts, rows = out.shape[0], out.shape[1] // 2
    for k in range(parts):
        out[k, :rows] = own_u[k * rows : (k + 1) * rows]
        out[k, rows:] = own_v[k * rows : (k + 1) * rows]


def scan_kernel(parts, rate, out):
    count, rows = parts.shape[0], parts.shape[1] // 2
    same, up, down = coarse(column(rate[...]))
    end_u, end_v = parts[0, :rows], parts[0, rows:]
    out[0, :rows], out[0, rows:] = end_u, end_v
    for k in range(1, count):
        end_u, end_v = (
            parts[k, :rows] + (same * end_u + up * end_v),
            parts[k, rows:] + (down * end_u + same * end_v),
        )
        out[k, :rows], out[k, rows:] = end_u, end_v


def on_device(flex, mass, coarse_rate, face_perm, start_u, start_v, load):
    a = flex[0]
    size, cases = start_u.shape[2:]
    half = size // 2
    subs, slices = lax.axis_size("sub"), lax.axis_size("tm")
    u, v, force = start_u[0, 0], start_v[0, 0], load[0, 0]
    right = [(s, s + 1) for s in range(subs - 1)]
    left = [(s + 1, s) for s in range(subs - 1)]
    face = ((half, cases), F32)
    small = ((8, cases), F32)
    whole = ((size, cases), F32)
    once = 2 * size * size * cases

    def swap(face_r, face_m):
        return lax.ppermute(face_r, "sub", right), lax.ppermute(face_m, "sub", left)

    y_l, y_r, y_m, onehot = call(
        start_kernel, "start", [face, face, face, ((half, half), BF16)], (a, u, v, force, mass, face_perm), once
    )
    held = None
    for step in range(2):
        from_left, from_right = swap(y_r, y_m)
        q_l, q_r, q_m, t_l, t_r, sums = call(
            first_kernel, "first", [face] * 5 + [small], (a, onehot, y_l, y_r, from_left, from_right), 2 * once
        )
        from_left, from_right = swap(q_r, q_m)
        s_l, s_r, spread = call(
            second_kernel,
            "second",
            [face] * 2 + [((subs, 8, cases), F32)],
            (a, onehot, q_l, q_r, from_left, from_right, sums),
            2 * once,
        )
        gathered = lax.all_to_all(spread, "sub", 0, 0)
        fields = (gathered, y_l, y_r, q_l, q_r, t_l, t_r, s_l, s_r)
        if step == 0:
            y_l, y_r, y_m, held = call(
                next_kernel, "next", [face] * 3 + [whole], (a, onehot) + fields + (u, v, force, mass), once
            )
    rows = size // slices
    mine = lax.dynamic_slice(coarse_rate, (0, lax.axis_index("tm") * rows), (1, rows))
    (parts,) = call(
        finish_kernel, "finish", [((slices, 2 * rows, cases), F32)], fields + (u, v, held, coarse_rate), size * cases * 20
    )
    parts = lax.all_to_all(parts, "tm", 0, 0)
    (ends,) = call(scan_kernel, "scan", [(parts.shape, F32)], (parts, mine), size * cases * 10)
    ends = lax.all_to_all(ends, "tm", 0, 0)
    end_u = ends[:, :rows].reshape(1, 1, size, cases)
    end_v = ends[:, rows:].reshape(1, 1, size, cases)
    return end_u, end_v


def solution(mesh):
    return jax.shard_map(
        on_device,
        mesh=mesh,
        in_specs=(
            P("sub", None, None),
            P("sub", None),
            P("sub", None),
            P("sub", None),
            P("tm", "sub", None, None),
            P("tm", "sub", None, None),
            P("tm", "sub", None, None),
        ),
        out_specs=(P("tm", "sub", None, None), P("tm", "sub", None, None)),
        check_vma=False,
    )
```

```python
import jax
import jax.numpy as jnp
from jax import lax
from jax.experimental import pallas as pl
from jax.experimental.pallas import tpu as pltpu
from jax.sharding import PartitionSpec as P

F32 = jnp.float32
BF16 = jnp.bfloat16
VMEM = pl.BlockSpec(memory_space=pltpu.VMEM)
ANY = pl.BlockSpec(memory_space=pl.ANY)
CHUNKS = 4


def call(kernel, name, outs, args, flops=0, in_specs=None, scratch=(), limit=24):
    moved = sum(a.size * a.dtype.itemsize for a in args)
    return pl.pallas_call(
        kernel,
        name=name,
        out_shape=[jax.ShapeDtypeStruct(shape, dtype) for shape, dtype in outs],
        in_specs=in_specs or [VMEM] * len(args),
        out_specs=[VMEM] * len(outs),
        scratch_shapes=scratch,
        compiler_params=pltpu.CompilerParams(vmem_limit_bytes=limit * 2**20),
        cost_estimate=pl.CostEstimate(flops=flops, bytes_accessed=moved, transcendentals=0),
    )(*args)


def pair(value):
    high = value.astype(BF16)
    return jnp.concatenate([high, (value - high.astype(F32)).astype(BF16)], axis=1)


def triple(value):
    high = value.astype(BF16)
    rest = value - high.astype(F32)
    middle = rest.astype(BF16)
    low = (rest - middle.astype(F32)).astype(BF16)
    return jnp.concatenate([high, middle, low], axis=1)


def fold(wide):
    return wide[:, :128] + wide[:, 128:256] + wide[:, 256:]


def to_multipliers(onehot, face):
    return fold(jnp.dot(onehot, triple(face), preferred_element_type=F32))


def to_left(onehot, block):
    return fold(lax.dot_general(onehot, triple(block), (((0,), (0,)), ((), ())), preferred_element_type=F32))


def column(row):
    width = row.shape[1]
    pieces = [jnp.transpose(jnp.broadcast_to(row[:, k : k + 128], (128, 128))) for k in range(0, width, 128)]
    return jnp.concatenate(pieces, axis=0)


def add_up(value):
    return jnp.sum(value, axis=0, keepdims=True)


def start_kernel(
    a_in, u_in, v_in, load_in, mass_in, perm_in, a, onehot, y_l, y_r, base, force, u, v, load, mass, perm, fields_sem, a_sem
):
    size = a.shape[0]
    half, rows = size // 2, size // CHUNKS
    small = [
        pltpu.make_async_copy(source, target, fields_sem.at[k])
        for k, (source, target) in enumerate(
            [(perm_in, perm), (mass_in, mass), (u_in, u), (v_in, v), (load_in, load)]
        )
    ]
    big = [
        pltpu.make_async_copy(a_in.at[pl.ds(k * rows, rows)], a.at[pl.ds(k * rows, rows)], a_sem.at[k])
        for k in range(CHUNKS)
    ]
    for copy in small + big:
        copy.start()
    small[0].wait()
    onehot[...] = (lax.broadcasted_iota(jnp.int32, (half, half), 0) == perm[...]).astype(F32).astype(BF16)
    for copy in small[1:]:
        copy.wait()
    weight = 2.0 * column(mass[...])
    outer = load[...].astype(F32)
    rhs = (outer + weight * (u[...] + v[...])).astype(BF16)
    before = 2.0 * u[...] + v[...]
    base[...] = before
    force[...] = outer - weight * before
    parts = []
    for k in range(CHUNKS):
        big[k].wait()
        parts.append(jnp.dot(a[k * rows : (k + 1) * rows], rhs, preferred_element_type=F32))
        if k == CHUNKS // 2 - 1:
            y_l[...] = to_multipliers(onehot[...], jnp.concatenate(parts, axis=0))
            parts = []
    y_r[...] = jnp.concatenate(parts, axis=0)


def prepare_kernel(a, onehot, force, mass, b, force_m, weight_m, turned):
    size = a.shape[0]
    half, rows = size // 2, size // CHUNKS
    hot = onehot[...]
    for k in range(CHUNKS):
        here = slice(k * rows, (k + 1) * rows)
        block = lax.dot_general(a[here, :half], hot, (((1,), (1,)), ((), ())), preferred_element_type=F32).astype(BF16)
        if k < CHUNKS // 2:
            turned[here] = block
        else:
            b[here, :half] = block
            b[here, half:] = a[here, half:]
    for k in range(CHUNKS):
        here = slice(k * rows, (k + 1) * rows)
        block = turned[:, here] if k < CHUNKS // 2 else a[:half, here]
        b[:half, here] = jnp.dot(hot, block, preferred_element_type=F32).astype(BF16)
    weight = 6.0 * column(mass[...])
    force_m[half:] = force[half:]
    force_m[:half] = to_multipliers(hot, force[:half])
    weight_m[half:] = weight[half:]
    weight_m[:half] = to_multipliers(hot, weight[:half])


def jump(f_l, f_r, from_left, from_right):
    sub = lax.axis_index("sub")
    left = jnp.where(sub == 0, 0.0, f_l[...] - from_left[...])
    right = jnp.where(sub == lax.axis_size("sub") - 1, 0.0, f_r[...] - from_right[...])
    return left, right


def first_kernel(b, y_l, y_r, from_left, from_right, q_l, q_r, t_l, t_r, sums):
    half = y_l.shape[0]
    left, right = jump(y_l, y_r, from_left, from_right)
    z = jnp.concatenate([pair(left), pair(right)], axis=0)
    wide = jnp.dot(b[...], z, preferred_element_type=F32)
    q = wide[:, :128]
    t = q + wide[:, 128:]
    q_l[...], q_r[...] = q[:half], q[half:]
    t_l[...], t_r[...] = t[:half], t[half:]
    rr = add_up(right * right)
    pw = add_up(left * q[:half]) + add_up(right * q[half:])
    sums[...] = jnp.concatenate([rr, pw, jnp.zeros((6, 128), F32)], axis=0)


def second_kernel(b, q_l, q_r, from_left, from_right, sums, s_l, s_r, spread):
    half = q_l.shape[0]
    left, right = jump(q_l, q_r, from_left, from_right)
    z = jnp.concatenate([pair(left), pair(right)], axis=0)
    wide = jnp.dot(b[...], z, preferred_element_type=F32)
    s = wide[:, :128] + wide[:, 128:]
    s_l[...], s_r[...] = s[:half], s[half:]
    ww = add_up(right * right)
    wfw = add_up(left * s[:half]) + add_up(right * s[half:])
    own = jnp.concatenate([sums[:2], ww, wfw, jnp.zeros((4, 128), F32)], axis=0)
    spread[...] = jnp.broadcast_to(own[None], spread.shape)


def corrected(gathered, y_l, y_r, q_l, q_r, t_l, t_r, s_l, s_r):
    total = jnp.sum(gathered[...], axis=0)
    rr, pw, ww, wfw = total[0:1], total[1:2], total[2:3], total[3:4]
    alpha = rr / pw
    ratio = ww / pw
    later = (alpha * alpha * ww - rr) / (alpha * alpha * (wfw - ww * ratio))
    gain = alpha * later

    def face(y, q, t, s):
        return y[...] - alpha * q[...] - gain * (ratio * t[...] - s[...])

    return face(y_l, q_l, t_l, s_l), face(y_r, q_r, t_r, s_r)


def next_kernel(b, gathered, y_l, y_r, q_l, q_r, t_l, t_r, s_l, s_r, force_m, weight_m, z_l, z_r, u_l, u_r):
    half = y_l.shape[0]
    left, right = corrected(gathered, y_l, y_r, q_l, q_r, t_l, t_r, s_l, s_r)
    u_l[...], u_r[...] = left, right
    rhs = (force_m[...] + weight_m[...] * jnp.concatenate([left, right], axis=0)).astype(BF16)
    y = jnp.dot(b[...], rhs, preferred_element_type=F32)
    z_l[...], z_r[...] = y[:half], y[half:]


def coarse(rate):
    scale = 1.0 / (1.0 + rate)
    return (1.0 - rate) * scale, 2.0 * scale, -2.0 * rate * scale


def early_kernel(onehot, u_l, u_r, base, u, v, rate, early_u, early_v, rate_own):
    tm = lax.axis_index("tm")
    half = u_l.shape[0]
    rates = column(rate[...])
    rate_own[...] = jnp.where(tm % 2 == 0, rates[:half], rates[half:])
    same, up, down = coarse(rates)
    later = jnp.concatenate([to_left(onehot[...], u_l[...]), u_r[...]], axis=0)
    early_u[...] = -jnp.where(tm == 0, 0.0, same * u[...] + up * v[...])
    early_v[...] = base[...] - 4.0 * later - jnp.where(tm == 0, 0.0, down * u[...] + same * v[...])


def finish_kernel(onehot, gathered, y_l, y_r, q_l, q_r, t_l, t_r, s_l, s_r, early_u, early_v, own, give):
    even = lax.axis_index("tm") % 2 == 0
    half = y_l.shape[0]
    left, right = corrected(gathered, y_l, y_r, q_l, q_r, t_l, t_r, s_l, s_r)
    left = to_left(onehot[...], left)
    for k, (early, factor) in enumerate([(early_u, 1.0), (early_v, 2.0)]):
        top = factor * left + early[:half]
        bottom = factor * right + early[half:]
        own[k] = jnp.where(even, top, bottom)
        give[k] = jnp.where(even, bottom, top)


def step_on(rate, state_u, state_v):
    same, up, down = coarse(rate)
    return same * state_u + up * state_v, down * state_u + same * state_v


def both_slices(own, got):
    even = lax.axis_index("tm") % 2 == 0
    return [jnp.where(even, own[k], got[k]) for k in range(2)], [jnp.where(even, got[k], own[k]) for k in range(2)]


def combine_kernel(own, got, rate_own, kept, ahead, across, behind, scratch):
    chip = lax.axis_index("tm") // 2
    chips = lax.axis_size("tm") // 2
    rows = kept.shape[1]
    first, second = both_slices(own, got)
    moved = step_on(rate_own[...], *first)
    for k in range(2):
        scratch[k] = second[k] + moved[k]
    for offset, out in enumerate([kept, ahead, across, behind]):
        start = pl.multiple_of(lax.rem(chip + offset, chips) * rows, rows)
        for k in range(2):
            out[k] = scratch[k, pl.ds(start, rows)]


def prefix_kernel(kept, from_1, from_2, from_3, rate_own, ahead, across, behind, mine, scratch):
    chip = lax.axis_index("tm") // 2
    chips = lax.axis_size("tm") // 2
    rows = kept.shape[1]
    for offset, arrived in enumerate([kept, from_1, from_2, from_3]):
        scratch[lax.rem(chip + chips - offset, chips)] = arrived[...]
    rate = rate_own[pl.ds(pl.multiple_of(chip * rows, rows), rows)]
    state = [scratch[0, k] for k in range(2)]
    for place in range(1, chips):
        after = [scratch[place, k] for k in range(2)]
        for k in range(2):
            scratch[place, k] = state[k]
        moved = step_on(rate, *step_on(rate, *state))
        state = [after[k] + moved[k] for k in range(2)]
    scratch[0] = jnp.zeros(scratch.shape[1:], F32)
    for offset, out in enumerate([mine, ahead, across, behind]):
        out[...] = scratch[lax.rem(chip + offset, chips)]


def end_kernel(mine, from_1, from_2, from_3, own, got, rate_own, stay, give, scratch):
    chip = lax.axis_index("tm") // 2
    chips = lax.axis_size("tm") // 2
    even = lax.axis_index("tm") % 2 == 0
    rows = mine.shape[1]
    for offset, arrived in enumerate([mine, from_1, from_2, from_3]):
        start = pl.multiple_of(lax.rem(chip + chips - offset, chips) * rows, rows)
        for k in range(2):
            scratch[k, pl.ds(start, rows)] = arrived[k]
    first, second = both_slices(own, got)
    rate = rate_own[...]
    moved = step_on(rate, scratch[0], scratch[1])
    first = [first[k] + moved[k] for k in range(2)]
    moved = step_on(rate, *first)
    second = [second[k] + moved[k] for k in range(2)]
    for k in range(2):
        stay[k] = jnp.where(even, first[k], second[k])
        give[k] = jnp.where(even, second[k], first[k])


def join_kernel(stay, got, end_u, end_v):
    even = lax.axis_index("tm") % 2 == 0
    half = stay.shape[1]
    for k, out in enumerate([end_u, end_v]):
        out[:half] = jnp.where(even, stay[k], got[k])
        out[half:] = jnp.where(even, got[k], stay[k])


def on_device(flex, mass, coarse_rate, face_perm, start_u, start_v, load):
    size, cases = start_u.shape[2:]
    half = size // 2
    subs, slices = lax.axis_size("sub"), lax.axis_size("tm")
    u, v, outer = start_u[0, 0], start_v[0, 0], load[0, 0]
    right = [(s, s + 1) for s in range(subs - 1)]
    left = [(s + 1, s) for s in range(subs - 1)]
    face = ((half, cases), F32)
    whole = ((size, cases), F32)
    square = ((size, size), BF16)
    once = 2 * size * size * cases

    def exchange(face_l, face_r):
        return lax.ppermute(face_r, "sub", right), lax.ppermute(face_l, "sub", left)

    a, onehot, y_l, y_r, base, force = call(
        start_kernel,
        "start",
        [square, ((half, half), BF16), face, face, whole, whole],
        (flex[0], u, v, outer, mass, face_perm),
        once,
        in_specs=[ANY] * 6,
        scratch=[
            pltpu.VMEM((size, cases), F32),
            pltpu.VMEM((size, cases), F32),
            pltpu.VMEM((size, cases), BF16),
            pltpu.VMEM((1, size), F32),
            pltpu.VMEM((1, half), jnp.int32),
            pltpu.SemaphoreType.DMA((5,)),
            pltpu.SemaphoreType.DMA((CHUNKS,)),
        ],
    )
    matrix = None
    for step in range(2):
        from_left, from_right = exchange(y_l, y_r)
        if step == 0:
            matrix, force_m, weight_m = call(
                prepare_kernel,
                "prepare",
                [square, whole, whole],
                (a, onehot, force, mass),
                8 * half**3 * 2,
                scratch=[pltpu.VMEM((half, half), BF16)],
            )
        else:
            early_u, early_v, rate_own = call(
                early_kernel, "early", [whole, whole, face], (onehot, u_l, u_r, base, u, v, coarse_rate), 3 * half * once // size
            )
        q_l, q_r, t_l, t_r, sums = call(
            first_kernel, "first", [face] * 4 + [((8, cases), F32)], (matrix, y_l, y_r, from_left, from_right), 2 * once
        )
        from_left, from_right = exchange(q_l, q_r)
        s_l, s_r, spread = call(
            second_kernel,
            "second",
            [face] * 2 + [((subs, 8, cases), F32)],
            (matrix, q_l, q_r, from_left, from_right, sums),
            2 * once,
        )
        gathered = lax.all_to_all(spread, "sub", 0, 0)
        fields = (gathered, y_l, y_r, q_l, q_r, t_l, t_r, s_l, s_r)
        if step == 0:
            y_l, y_r, u_l, u_r = call(next_kernel, "next", [face] * 4, (matrix,) + fields + (force_m, weight_m), once)

    chips = slices // 2
    rows = half // chips
    two = ((2, half, cases), F32)
    block = ((2, rows, cases), F32)
    light = size * cases * 10

    def swap(value):
        return lax.ppermute(value, "tm", [(t, t ^ 1) for t in range(slices)])

    own, give = call(finish_kernel, "finish", [two, two], (onehot,) + fields + (early_u, early_v), light)
    got = swap(give)
    kept, *out = call(
        combine_kernel, "combine", [block] * 4, (own, got, rate_own), light, scratch=[pltpu.VMEM((2, half, cases), F32)]
    )
    arrived = [
        lax.ppermute(out[k - 1], "tm", [(t, (t + 2 * k) % slices) for t in range(slices - 2)]) for k in range(1, chips)
    ]
    *out, mine = call(
        prefix_kernel,
        "prefix",
        [block] * 4,
        (kept, *arrived, rate_own),
        light,
        scratch=[pltpu.VMEM((chips, 2, rows, cases), F32)],
    )
    arrived = [
        lax.ppermute(out[k - 1], "tm", [(t, (t + 2 * k) % slices) for t in range(slices) if (t + 2 * k) % slices > 1])
        for k in range(1, chips)
    ]
    stay, give = call(
        end_kernel,
        "end",
        [two, two],
        (mine, *arrived, own, got, rate_own),
        light,
        scratch=[pltpu.VMEM((2, half, cases), F32)],
    )
    end_u, end_v = call(join_kernel, "join", [whole, whole], (stay, swap(give)), light)
    return end_u[None, None], end_v[None, None]


def solution(mesh):
    return jax.shard_map(
        on_device,
        mesh=mesh,
        in_specs=(
            P("sub", None, None),
            P("sub", None),
            P("sub", None),
            P("sub", None),
            P("tm", "sub", None, None),
            P("tm", "sub", None, None),
            P("tm", "sub", None, None),
        ),
        out_specs=(P("tm", "sub", None, None), P("tm", "sub", None, None)),
        check_vma=False,
    )
```

```python
import jax
import jax.numpy as jnp
from jax import lax
from jax.experimental import pallas as pl
from jax.experimental.pallas import tpu as pltpu
from jax.sharding import PartitionSpec as P

F32 = jnp.float32
BF16 = jnp.bfloat16
VMEM = pl.BlockSpec(memory_space=pltpu.VMEM)
HBM = pl.BlockSpec(memory_space=pltpu.HBM)
CHUNKS = 4


def call(kernel, name, outs, args, flops=0, in_specs=None, scratch=(), limit=12, space=pltpu.VMEM):
    moved = sum(a.size * a.dtype.itemsize for a in args)
    return pl.pallas_call(
        kernel,
        name=name,
        out_shape=[space(shape, dtype) for shape, dtype in outs],
        in_specs=in_specs or [VMEM] * len(args),
        out_specs=[VMEM] * len(outs),
        scratch_shapes=scratch,
        compiler_params=pltpu.CompilerParams(vmem_limit_bytes=limit * 2**20),
        cost_estimate=pl.CostEstimate(flops=flops, bytes_accessed=moved, transcendentals=0),
    )(*args)


def pair(value):
    high = value.astype(BF16)
    return jnp.concatenate([high, (value - high.astype(F32)).astype(BF16)], axis=1)


def triple(value):
    high = value.astype(BF16)
    rest = value - high.astype(F32)
    middle = rest.astype(BF16)
    low = (rest - middle.astype(F32)).astype(BF16)
    return jnp.concatenate([high, middle, low], axis=1)


def fold(wide):
    return wide[:, :128] + wide[:, 128:256] + wide[:, 256:]


def to_multipliers(onehot, face):
    return fold(jnp.dot(onehot, triple(face), preferred_element_type=F32))


def to_left(onehot, block):
    return fold(lax.dot_general(onehot, triple(block), (((0,), (0,)), ((), ())), preferred_element_type=F32))


def column(row):
    width = row.shape[1]
    pieces = [jnp.transpose(jnp.broadcast_to(row[:, k : k + 128], (128, 128))) for k in range(0, width, 128)]
    return jnp.concatenate(pieces, axis=0)


def add_up(value):
    return jnp.sum(value, axis=0, keepdims=True)


def start_kernel(
    a_in, u_in, v_in, load_in, mass_in, perm_in, a, onehot, y_l, y_r, base, force, u, v, load, mass, perm, fields_sem, a_sem
):
    size = a.shape[0]
    half, rows = size // 2, size // CHUNKS
    small = [
        pltpu.make_async_copy(source, target, fields_sem.at[k])
        for k, (source, target) in enumerate(
            [(perm_in, perm), (mass_in, mass), (u_in, u), (v_in, v), (load_in, load)]
        )
    ]
    big = [
        pltpu.make_async_copy(a_in.at[pl.ds(k * rows, rows)], a.at[pl.ds(k * rows, rows)], a_sem.at[k])
        for k in range(CHUNKS)
    ]
    for copy in small + big:
        copy.start()
    small[0].wait()
    onehot[...] = (lax.broadcasted_iota(jnp.int32, (half, half), 0) == perm[...]).astype(F32).astype(BF16)
    for copy in small[1:]:
        copy.wait()
    weight = 2.0 * column(mass[...])
    outer = load[...].astype(F32)
    rhs = (outer + weight * (u[...] + v[...])).astype(BF16)
    before = 2.0 * u[...] + v[...]
    base[...] = before
    force[...] = outer - weight * before
    parts = []
    for k in range(CHUNKS):
        big[k].wait()
        parts.append(jnp.dot(a[k * rows : (k + 1) * rows], rhs, preferred_element_type=F32))
        if k == CHUNKS // 2 - 1:
            y_l[...] = to_multipliers(onehot[...], jnp.concatenate(parts, axis=0))
            parts = []
    y_r[...] = jnp.concatenate(parts, axis=0)


def prepare_kernel(a, onehot, b, order, turned):
    order[...] = jnp.zeros(order.shape, F32)
    size = a.shape[0]
    half, rows = size // 2, size // CHUNKS
    hot = onehot[...]
    for k in range(CHUNKS):
        here = slice(k * rows, (k + 1) * rows)
        block = lax.dot_general(a[here, :half], hot, (((1,), (1,)), ((), ())), preferred_element_type=F32).astype(BF16)
        if k < CHUNKS // 2:
            turned[here] = block
        else:
            b[here, :half] = block
            b[here, half:] = a[here, half:]
    for k in range(CHUNKS):
        here = slice(k * rows, (k + 1) * rows)
        block = turned[:, here] if k < CHUNKS // 2 else a[:half, here]
        b[:half, here] = jnp.dot(hot, block, preferred_element_type=F32).astype(BF16)


def ready_kernel(onehot, force, mass_in, rate_in, u_in, v_in, base, sums_in, force_m, weight_m, early_u, early_v, rate_own, sums, mass, rate, u, v, sem):
    copies = [
        pltpu.make_async_copy(source, target, sem.at[k]) for k, (source, target) in enumerate([(mass_in, mass), (rate_in, rate), (u_in, u), (v_in, v)])
    ]
    for copy in copies:
        copy.start()
    sums[...] = sums_in[...]
    hot = onehot[...]
    half = hot.shape[0]
    copies[0].wait()
    weight = 6.0 * column(mass[...])
    force_m[half:] = force[half:]
    force_m[:half] = to_multipliers(hot, force[:half])
    weight_m[half:] = weight[half:]
    weight_m[:half] = to_multipliers(hot, weight[:half])
    for copy in copies[1:]:
        copy.wait()
    tm = lax.axis_index("tm")
    rates = column(rate[...])
    rate_own[...] = jnp.where(tm % 2 == 0, rates[:half], rates[half:])
    same, up, down = coarse(rates)
    early_u[...] = -jnp.where(tm == 0, 0.0, same * u[...] + up * v[...])
    early_v[...] = base[...] - jnp.where(tm == 0, 0.0, down * u[...] + same * v[...])


def jump(f_l, f_r, from_left, from_right):
    sub = lax.axis_index("sub")
    left = jnp.where(sub == 0, 0.0, f_l[...] - from_left[...])
    right = jnp.where(sub == lax.axis_size("sub") - 1, 0.0, f_r[...] - from_right[...])
    return left, right


def first_kernel(b, y_l, y_r, from_left, from_right, order, q_l, q_r, t_l, t_r, sums):
    half = y_l.shape[0]
    left, right = jump(y_l, y_r, from_left, from_right)
    z = jnp.concatenate([pair(left), pair(right)], axis=0)
    wide = jnp.dot(b[...], z, preferred_element_type=F32)
    q = wide[:, :128]
    t = q + wide[:, 128:]
    q_l[...], q_r[...] = q[:half], q[half:]
    t_l[...], t_r[...] = t[:half], t[half:]
    rr = add_up(right * right)
    pw = add_up(left * q[:half]) + add_up(right * q[half:])
    sums[...] = jnp.concatenate([rr, pw, order[2:]], axis=0)


def second_kernel(b, q_l, q_r, from_left, from_right, sums, s_l, s_r, spread):
    half = q_l.shape[0]
    left, right = jump(q_l, q_r, from_left, from_right)
    z = jnp.concatenate([pair(left), pair(right)], axis=0)
    wide = jnp.dot(b[...], z, preferred_element_type=F32)
    s = wide[:, :128] + wide[:, 128:]
    s_l[...], s_r[...] = s[:half], s[half:]
    ww = add_up(right * right)
    wfw = add_up(left * s[:half]) + add_up(right * s[half:])
    own = jnp.concatenate([sums[:2], ww, wfw, jnp.zeros((4, 128), F32)], axis=0)
    spread[...] = jnp.broadcast_to(own[None], spread.shape)


def corrected(gathered, y_l, y_r, q_l, q_r, t_l, t_r, s_l, s_r):
    total = jnp.sum(gathered[...], axis=0)
    rr, pw, ww, wfw = total[0:1], total[1:2], total[2:3], total[3:4]
    alpha = rr / pw
    ratio = ww / pw
    later = (alpha * alpha * ww - rr) / (alpha * alpha * (wfw - ww * ratio))
    gain = alpha * later

    def face(y, q, t, s):
        return y[...] - alpha * q[...] - gain * (ratio * t[...] - s[...])

    return face(y_l, q_l, t_l, s_l), face(y_r, q_r, t_r, s_r)


def next_kernel(b, gathered, y_l, y_r, q_l, q_r, t_l, t_r, s_l, s_r, force_m, weight_m, z_l, z_r, u_l, u_r):
    half = y_l.shape[0]
    left, right = corrected(gathered, y_l, y_r, q_l, q_r, t_l, t_r, s_l, s_r)
    u_l[...], u_r[...] = left, right
    rhs = (force_m[...] + weight_m[...] * jnp.concatenate([left, right], axis=0)).astype(BF16)
    y = jnp.dot(b[...], rhs, preferred_element_type=F32)
    z_l[...], z_r[...] = y[:half], y[half:]


def coarse(rate):
    scale = 1.0 / (1.0 + rate)
    return (1.0 - rate) * scale, 2.0 * scale, -2.0 * rate * scale


def early_kernel(onehot, u_l, u_r, early_in, early_v, order):
    order[...] = jnp.zeros(order.shape, F32)
    half = u_l.shape[0]
    early_v[:half] = early_in[:half] - 4.0 * to_left(onehot[...], u_l[...])
    early_v[half:] = early_in[half:] - 4.0 * u_r[...]


def finish_kernel(onehot, gathered, y_l, y_r, q_l, q_r, t_l, t_r, s_l, s_r, early_u, early_v, own, give):
    even = lax.axis_index("tm") % 2 == 0
    half = y_l.shape[0]
    left, right = corrected(gathered, y_l, y_r, q_l, q_r, t_l, t_r, s_l, s_r)
    left = to_left(onehot[...], left)
    for k, (early, factor) in enumerate([(early_u, 1.0), (early_v, 2.0)]):
        top = factor * left + early[:half]
        bottom = factor * right + early[half:]
        own[k] = jnp.where(even, top, bottom)
        give[k] = jnp.where(even, bottom, top)


def step_on(rate, state_u, state_v):
    same, up, down = coarse(rate)
    return same * state_u + up * state_v, down * state_u + same * state_v


def both_slices(own, got):
    even = lax.axis_index("tm") % 2 == 0
    return [jnp.where(even, own[k], got[k]) for k in range(2)], [jnp.where(even, got[k], own[k]) for k in range(2)]


def combine_kernel(own, got, rate_own, kept, ahead, across, behind, scratch):
    chip = lax.axis_index("tm") // 2
    chips = lax.axis_size("tm") // 2
    rows = kept.shape[1]
    first, second = both_slices(own, got)
    moved = step_on(rate_own[...], *first)
    for k in range(2):
        scratch[k] = second[k] + moved[k]
    for offset, out in enumerate([kept, ahead, across, behind]):
        start = pl.multiple_of(lax.rem(chip + offset, chips) * rows, rows)
        for k in range(2):
            out[k] = scratch[k, pl.ds(start, rows)]


def prefix_kernel(kept, from_1, from_2, from_3, rate_own, ahead, across, behind, mine, scratch):
    chip = lax.axis_index("tm") // 2
    chips = lax.axis_size("tm") // 2
    rows = kept.shape[1]
    for offset, arrived in enumerate([kept, from_1, from_2, from_3]):
        scratch[lax.rem(chip + chips - offset, chips)] = arrived[...]
    rate = rate_own[pl.ds(pl.multiple_of(chip * rows, rows), rows)]
    state = [scratch[0, k] for k in range(2)]
    for place in range(1, chips):
        after = [scratch[place, k] for k in range(2)]
        for k in range(2):
            scratch[place, k] = state[k]
        moved = step_on(rate, *step_on(rate, *state))
        state = [after[k] + moved[k] for k in range(2)]
    scratch[0] = jnp.zeros(scratch.shape[1:], F32)
    for offset, out in enumerate([mine, ahead, across, behind]):
        out[...] = scratch[lax.rem(chip + offset, chips)]


def end_kernel(mine, from_1, from_2, from_3, own, got, rate_own, stay, give, scratch):
    chip = lax.axis_index("tm") // 2
    chips = lax.axis_size("tm") // 2
    even = lax.axis_index("tm") % 2 == 0
    rows = mine.shape[1]
    for offset, arrived in enumerate([mine, from_1, from_2, from_3]):
        start = pl.multiple_of(lax.rem(chip + chips - offset, chips) * rows, rows)
        for k in range(2):
            scratch[k, pl.ds(start, rows)] = arrived[k]
    first, second = both_slices(own, got)
    rate = rate_own[...]
    moved = step_on(rate, scratch[0], scratch[1])
    first = [first[k] + moved[k] for k in range(2)]
    moved = step_on(rate, *first)
    second = [second[k] + moved[k] for k in range(2)]
    for k in range(2):
        stay[k] = jnp.where(even, first[k], second[k])
        give[k] = jnp.where(even, second[k], first[k])


def join_kernel(stay, got, end_u, end_v):
    even = lax.axis_index("tm") % 2 == 0
    half = stay.shape[1]
    for k, out in enumerate([end_u, end_v]):
        out[:half] = jnp.where(even, stay[k], got[k])
        out[half:] = jnp.where(even, got[k], stay[k])


def on_device(flex, mass, coarse_rate, face_perm, start_u, start_v, load):
    size, cases = start_u.shape[2:]
    half = size // 2
    subs, slices = lax.axis_size("sub"), lax.axis_size("tm")
    flex, mass, coarse_rate, face_perm, u, v, outer = [
        pltpu.with_memory_space_constraint(value, pltpu.HBM)
        for value in (flex[0], mass, coarse_rate, face_perm, start_u[0, 0], start_v[0, 0], load[0, 0])
    ]
    right = [(s, s + 1) for s in range(subs - 1)]
    left = [(s + 1, s) for s in range(subs - 1)]
    face = ((half, cases), F32)
    whole = ((size, cases), F32)
    small = ((8, cases), F32)
    square = ((size, size), BF16)
    once = 2 * size * size * cases

    def exchange(face_l, face_r):
        return lax.ppermute(face_r, "sub", right), lax.ppermute(face_l, "sub", left)

    a, onehot, y_l, y_r, base, force = call(
        start_kernel,
        "start",
        [square, ((half, half), BF16), face, face, whole, whole],
        (flex, u, v, outer, mass, face_perm),
        once,
        in_specs=[HBM] * 6,
        scratch=[
            pltpu.VMEM((size, cases), F32),
            pltpu.VMEM((size, cases), F32),
            pltpu.VMEM((size, cases), BF16),
            pltpu.VMEM((1, size), F32),
            pltpu.VMEM((1, half), jnp.int32),
            pltpu.SemaphoreType.DMA((5,)),
            pltpu.SemaphoreType.DMA((CHUNKS,)),
        ],
    )
    matrix = None
    for step in range(2):
        from_left, from_right = exchange(y_l, y_r)
        if step == 0:
            matrix, order = call(
                prepare_kernel, "prepare", [square, small], (a, onehot), 8 * half**3, scratch=[pltpu.VMEM((half, half), BF16)]
            )
        else:
            early_v, order = call(early_kernel, "early", [whole, small], (onehot, u_l, u_r, early_v), 2 * half * half * 3 * cases)
        q_l, q_r, t_l, t_r, sums = call(
            first_kernel, "first", [face] * 4 + [small], (matrix, y_l, y_r, from_left, from_right, order), 2 * once
        )
        from_left, from_right = exchange(q_l, q_r)
        if step == 0:
            force_m, weight_m, early_u, early_v, rate_own, sums = call(
                ready_kernel,
                "ready",
                [whole] * 4 + [face, small],
                (onehot, force, mass, coarse_rate, u, v, base, sums),
                2 * half * half * 6 * cases,
                in_specs=[VMEM] * 2 + [HBM] * 4 + [VMEM] * 2,
                scratch=[
                    pltpu.VMEM((1, size), F32),
                    pltpu.VMEM((1, size), F32),
                    pltpu.VMEM((size, cases), F32),
                    pltpu.VMEM((size, cases), F32),
                    pltpu.SemaphoreType.DMA((4,)),
                ],
            )
        s_l, s_r, spread = call(
            second_kernel,
            "second",
            [face] * 2 + [((subs, 8, cases), F32)],
            (matrix, q_l, q_r, from_left, from_right, sums),
            2 * once,
        )
        gathered = lax.all_to_all(spread, "sub", 0, 0)
        fields = (gathered, y_l, y_r, q_l, q_r, t_l, t_r, s_l, s_r)
        if step == 0:
            y_l, y_r, u_l, u_r = call(next_kernel, "next", [face] * 4, (matrix,) + fields + (force_m, weight_m), once)

    chips = slices // 2
    rows = half // chips
    two = ((2, half, cases), F32)
    block = ((2, rows, cases), F32)
    light = size * cases * 10

    def swap(value):
        return lax.ppermute(value, "tm", [(t, t ^ 1) for t in range(slices)])

    own, give = call(finish_kernel, "finish", [two, two], (onehot,) + fields + (early_u, early_v), light)
    got = swap(give)
    kept, *out = call(
        combine_kernel, "combine", [block] * 4, (own, got, rate_own), light, scratch=[pltpu.VMEM((2, half, cases), F32)]
    )
    arrived = [
        lax.ppermute(out[k - 1], "tm", [(t, (t + 2 * k) % slices) for t in range(slices - 2)]) for k in range(1, chips)
    ]
    *out, mine = call(
        prefix_kernel,
        "prefix",
        [block] * 4,
        (kept, *arrived, rate_own),
        light,
        scratch=[pltpu.VMEM((chips, 2, rows, cases), F32)],
    )
    arrived = [
        lax.ppermute(out[k - 1], "tm", [(t, (t + 2 * k) % slices) for t in range(slices) if (t + 2 * k) % slices > 1])
        for k in range(1, chips)
    ]
    stay, give = call(
        end_kernel,
        "end",
        [two, two],
        (mine, *arrived, own, got, rate_own),
        light,
        scratch=[pltpu.VMEM((2, half, cases), F32)],
    )
    end_u, end_v = call(join_kernel, "join", [whole, whole], (stay, swap(give)), light, space=jax.ShapeDtypeStruct)
    return end_u[None, None], end_v[None, None]


def solution(mesh):
    return jax.shard_map(
        on_device,
        mesh=mesh,
        in_specs=(
            P("sub", None, None),
            P("sub", None),
            P("sub", None),
            P("sub", None),
            P("tm", "sub", None, None),
            P("tm", "sub", None, None),
            P("tm", "sub", None, None),
        ),
        out_specs=(P("tm", "sub", None, None), P("tm", "sub", None, None)),
        check_vma=False,
    )
```

```python
import jax
import jax.numpy as jnp
from jax import lax
from jax.experimental import pallas as pl
from jax.experimental.pallas import tpu as pltpu
from jax.sharding import PartitionSpec as P

F32 = jnp.float32
BF16 = jnp.bfloat16
VMEM = pl.BlockSpec(memory_space=pltpu.VMEM)
HBM = pl.BlockSpec(memory_space=pltpu.HBM)
CHUNKS = 4


def call(kernel, name, outs, args, flops=0, in_specs=None, scratch=(), limit=12, space=pltpu.VMEM):
    moved = sum(a.size * a.dtype.itemsize for a in args)
    return pl.pallas_call(
        kernel,
        name=name,
        out_shape=[space(shape, dtype) for shape, dtype in outs],
        in_specs=in_specs or [VMEM] * len(args),
        out_specs=[VMEM] * len(outs),
        scratch_shapes=scratch,
        compiler_params=pltpu.CompilerParams(vmem_limit_bytes=limit * 2**20),
        cost_estimate=pl.CostEstimate(flops=flops, bytes_accessed=moved, transcendentals=0),
    )(*args)


def pair(value):
    high = value.astype(BF16)
    return jnp.concatenate([high, (value - high.astype(F32)).astype(BF16)], axis=1)


def triple(value):
    high = value.astype(BF16)
    rest = value - high.astype(F32)
    middle = rest.astype(BF16)
    low = (rest - middle.astype(F32)).astype(BF16)
    return jnp.concatenate([high, middle, low], axis=1)


def fold(wide):
    return wide[:, :128] + wide[:, 128:256] + wide[:, 256:]


def to_multipliers(onehot, face):
    return fold(jnp.dot(onehot, triple(face), preferred_element_type=F32))


def to_left(onehot, block):
    return fold(lax.dot_general(onehot, triple(block), (((0,), (0,)), ((), ())), preferred_element_type=F32))


def column(row):
    width = row.shape[1]
    pieces = [jnp.transpose(jnp.broadcast_to(row[:, k : k + 128], (128, 128))) for k in range(0, width, 128)]
    return jnp.concatenate(pieces, axis=0)


def add_up(value):
    return jnp.sum(value, axis=0, keepdims=True)


def is_even():
    return lax.rem(lax.axis_index("sub"), 2) == 0


def by_pairs(left, right):
    even = is_even()
    return jnp.where(even, right, left), jnp.where(even, left, right)


def by_sides(face_a, face_b):
    even = is_even()
    return jnp.where(even, face_b, face_a), jnp.where(even, face_a, face_b)


def start_kernel(
    a_in, u_in, v_in, load_in, mass_in, perm_in, a, onehot, y_a, y_b, base, force, u, v, load, mass, perm, fields_sem, a_sem
):
    size = a.shape[0]
    half, rows = size // 2, size // CHUNKS
    small = [
        pltpu.make_async_copy(source, target, fields_sem.at[k])
        for k, (source, target) in enumerate(
            [(perm_in, perm), (mass_in, mass), (u_in, u), (v_in, v), (load_in, load)]
        )
    ]
    big = [
        pltpu.make_async_copy(a_in.at[pl.ds(k * rows, rows)], a.at[pl.ds(k * rows, rows)], a_sem.at[k])
        for k in range(CHUNKS)
    ]
    for copy in small:
        copy.start()
    small[0].wait()
    onehot[...] = (lax.broadcasted_iota(jnp.int32, (half, half), 0) == perm[...]).astype(F32).astype(BF16)
    for copy in small[1:]:
        copy.wait()
    for copy in big:
        copy.start()
    weight = 2.0 * column(mass[...])
    outer = load[...].astype(F32)
    rhs = (outer + weight * (u[...] + v[...])).astype(BF16)
    before = 2.0 * u[...] + v[...]
    base[...] = before
    force[...] = outer - weight * before
    faces = []
    for first in (0, CHUNKS // 2):
        parts = []
        for k in range(first, first + CHUNKS // 2):
            big[k].wait()
            parts.append(jnp.dot(a[k * rows : (k + 1) * rows], rhs, preferred_element_type=F32))
        faces.append(jnp.concatenate(parts, axis=0))
        if first == 0:
            faces[0] = to_multipliers(onehot[...], faces[0])
    y_a[...], y_b[...] = by_pairs(*faces)


def prepare_kernel(a, onehot, b, order, turned):
    order[...] = jnp.zeros(order.shape, F32)
    size = a.shape[0]
    half, rows = size // 2, size // CHUNKS
    hot = onehot[...]
    odd = lax.rem(lax.axis_index("sub"), 2)

    def left(offset, count):
        return pl.ds(pl.multiple_of((1 - odd) * half + offset, rows), count)

    def right(offset, count):
        return pl.ds(pl.multiple_of(odd * half + offset, rows), count)

    for k in range(CHUNKS):
        here = slice(k * rows, (k + 1) * rows)
        block = lax.dot_general(a[here, :half], hot, (((1,), (1,)), ((), ())), preferred_element_type=F32).astype(BF16)
        if k < CHUNKS // 2:
            turned[here] = block
        else:
            down = right(k * rows - half, rows)
            b[down, left(0, half)] = block
            b[down, right(0, half)] = a[here, half:]
    for k in range(CHUNKS):
        here = slice(k * rows, (k + 1) * rows)
        if k < CHUNKS // 2:
            block, across = turned[:, here], left(k * rows, rows)
        else:
            block, across = a[:half, here], right(k * rows - half, rows)
        b[left(0, half), across] = jnp.dot(hot, block, preferred_element_type=F32).astype(BF16)


def ready_kernel(onehot, force, mass_in, rate_in, u_in, v_in, base, sums_in, force_m, weight_m, early_u, early_v, rate_own, sums, mass, rate, u, v, sem):
    copies = [
        pltpu.make_async_copy(source, target, sem.at[k]) for k, (source, target) in enumerate([(mass_in, mass), (rate_in, rate), (u_in, u), (v_in, v)])
    ]
    for copy in copies:
        copy.start()
    sums[...] = sums_in[...]
    hot = onehot[...]
    half = hot.shape[0]
    copies[0].wait()
    weight = 6.0 * column(mass[...])
    force_m[:half], force_m[half:] = by_pairs(to_multipliers(hot, force[:half]), force[half:])
    weight_m[:half], weight_m[half:] = by_pairs(to_multipliers(hot, weight[:half]), weight[half:])
    for copy in copies[1:]:
        copy.wait()
    tm = lax.axis_index("tm")
    rates = column(rate[...])
    rate_own[...] = jnp.where(tm % 2 == 0, rates[:half], rates[half:])
    same, up, down = coarse(rates)
    early_u[...] = -jnp.where(tm == 0, 0.0, same * u[...] + up * v[...])
    early_v[...] = base[...] - jnp.where(tm == 0, 0.0, down * u[...] + same * v[...])


def jump(f_a, f_b, from_a, from_b):
    sub = lax.axis_index("sub")
    alone = jnp.logical_or(sub == 0, sub == lax.axis_size("sub") - 1)
    return f_a[...] - from_a[...], jnp.where(alone, 0.0, f_b[...] - from_b[...])


def first_kernel(b, y_a, y_b, from_a, from_b, order, q_a, q_b, t_a, t_b, sums):
    half = y_a.shape[0]
    r_a, r_b = jump(y_a, y_b, from_a, from_b)
    z = jnp.concatenate([pair(r_a), pair(r_b)], axis=0)
    wide = jnp.dot(b[...], z, preferred_element_type=F32)
    q = wide[:, :128]
    t = q + wide[:, 128:]
    q_a[...], q_b[...] = q[:half], q[half:]
    t_a[...], t_b[...] = t[:half], t[half:]
    rr = 0.5 * (add_up(r_a * r_a) + add_up(r_b * r_b))
    pw = add_up(r_a * q[:half]) + add_up(r_b * q[half:])
    sums[...] = jnp.concatenate([rr, pw, order[2:]], axis=0)


def second_kernel(b, q_a, q_b, from_a, from_b, sums, s_a, s_b, spread):
    half = q_a.shape[0]
    w_a, w_b = jump(q_a, q_b, from_a, from_b)
    z = jnp.concatenate([pair(w_a), pair(w_b)], axis=0)
    wide = jnp.dot(b[...], z, preferred_element_type=F32)
    s = wide[:, :128] + wide[:, 128:]
    s_a[...], s_b[...] = s[:half], s[half:]
    ww = 0.5 * (add_up(w_a * w_a) + add_up(w_b * w_b))
    wfw = add_up(w_a * s[:half]) + add_up(w_b * s[half:])
    own = jnp.concatenate([sums[:2], ww, wfw, jnp.zeros((4, 128), F32)], axis=0)
    spread[...] = jnp.broadcast_to(own[None], spread.shape)


def corrected(gathered, y_a, y_b, q_a, q_b, t_a, t_b, s_a, s_b):
    total = jnp.sum(gathered[...], axis=0)
    rr, pw, ww, wfw = total[0:1], total[1:2], total[2:3], total[3:4]
    alpha = rr / pw
    ratio = ww / pw
    later = (alpha * alpha * ww - rr) / (alpha * alpha * (wfw - ww * ratio))
    gain = alpha * later

    def face(y, q, t, s):
        return y[...] - alpha * q[...] - gain * (ratio * t[...] - s[...])

    return face(y_a, q_a, t_a, s_a), face(y_b, q_b, t_b, s_b)


def next_kernel(b, gathered, y_a, y_b, q_a, q_b, t_a, t_b, s_a, s_b, force_m, weight_m, z_a, z_b, u_a, u_b):
    half = y_a.shape[0]
    new_a, new_b = corrected(gathered, y_a, y_b, q_a, q_b, t_a, t_b, s_a, s_b)
    u_a[...], u_b[...] = new_a, new_b
    rhs = (force_m[...] + weight_m[...] * jnp.concatenate([new_a, new_b], axis=0)).astype(BF16)
    y = jnp.dot(b[...], rhs, preferred_element_type=F32)
    z_a[...], z_b[...] = y[:half], y[half:]


def coarse(rate):
    scale = 1.0 / (1.0 + rate)
    return (1.0 - rate) * scale, 2.0 * scale, -2.0 * rate * scale


def early_kernel(onehot, u_a, u_b, early_in, early_v, order):
    order[...] = jnp.zeros(order.shape, F32)
    half = u_a.shape[0]
    left, right = by_sides(u_a[...], u_b[...])
    early_v[:half] = early_in[:half] - 4.0 * to_left(onehot[...], left)
    early_v[half:] = early_in[half:] - 4.0 * right


def finish_kernel(onehot, gathered, y_a, y_b, q_a, q_b, t_a, t_b, s_a, s_b, early_u, early_v, own, give):
    even = lax.axis_index("tm") % 2 == 0
    half = y_a.shape[0]
    left, right = by_sides(*corrected(gathered, y_a, y_b, q_a, q_b, t_a, t_b, s_a, s_b))
    left = to_left(onehot[...], left)
    for k, (early, factor) in enumerate([(early_u, 1.0), (early_v, 2.0)]):
        top = factor * left + early[:half]
        bottom = factor * right + early[half:]
        own[k] = jnp.where(even, top, bottom)
        give[k] = jnp.where(even, bottom, top)


def step_on(rate, state_u, state_v):
    same, up, down = coarse(rate)
    return same * state_u + up * state_v, down * state_u + same * state_v


def both_slices(own, got):
    even = lax.axis_index("tm") % 2 == 0
    return [jnp.where(even, own[k], got[k]) for k in range(2)], [jnp.where(even, got[k], own[k]) for k in range(2)]


def combine_kernel(own, got, rate_own, blocks):
    rows = blocks.shape[2]
    first, second = both_slices(own, got)
    moved = step_on(rate_own[...], *first)
    for k in range(2):
        both = second[k] + moved[k]
        for place in range(blocks.shape[0]):
            blocks[place, k] = both[place * rows : (place + 1) * rows]


def prefix_kernel(blocks, rate_own, states):
    rows = blocks.shape[2]
    chip = lax.axis_index("tm") // 2
    rate = rate_own[pl.ds(pl.multiple_of(chip * rows, rows), rows)]
    states[0] = jnp.zeros(states.shape[1:], F32)
    state = [blocks[0, k] for k in range(2)]
    for place in range(1, blocks.shape[0]):
        for k in range(2):
            states[place, k] = state[k]
        if place + 1 < blocks.shape[0]:
            moved = step_on(rate, *step_on(rate, *state))
            state = [blocks[place, k] + moved[k] for k in range(2)]


def end_kernel(states, own, got, rate_own, stay, give):
    even = lax.axis_index("tm") % 2 == 0
    first, second = both_slices(own, got)
    rate = rate_own[...]
    entering = [jnp.concatenate([states[place, k] for place in range(states.shape[0])], axis=0) for k in range(2)]
    moved = step_on(rate, *entering)
    first = [first[k] + moved[k] for k in range(2)]
    moved = step_on(rate, *first)
    second = [second[k] + moved[k] for k in range(2)]
    for k in range(2):
        stay[k] = jnp.where(even, first[k], second[k])
        give[k] = jnp.where(even, second[k], first[k])


def join_kernel(stay, got, end_u, end_v):
    even = lax.axis_index("tm") % 2 == 0
    half = stay.shape[1]
    for k, out in enumerate([end_u, end_v]):
        out[:half] = jnp.where(even, stay[k], got[k])
        out[half:] = jnp.where(even, got[k], stay[k])


def on_device(flex, mass, coarse_rate, face_perm, start_u, start_v, load):
    size, cases = start_u.shape[2:]
    half = size // 2
    subs, slices = lax.axis_size("sub"), lax.axis_size("tm")
    flex, mass, coarse_rate, face_perm, u, v, outer = [
        pltpu.with_memory_space_constraint(value, pltpu.HBM)
        for value in (flex[0], mass, coarse_rate, face_perm, start_u[0, 0], start_v[0, 0], load[0, 0])
    ]
    pairs = [[p for s in range(k, subs - 1, 2) for p in ((s, s + 1), (s + 1, s))] for k in range(2)]
    face = ((half, cases), F32)
    whole = ((size, cases), F32)
    small = ((8, cases), F32)
    square = ((size, size), BF16)
    once = 2 * size * size * cases

    def exchange(face_a, face_b):
        from_b = lax.ppermute(face_b, "sub", pairs[1])
        return lax.ppermute(face_a, "sub", pairs[0]), from_b

    a, onehot, y_a, y_b, base, force = call(
        start_kernel,
        "start",
        [square, ((half, half), BF16), face, face, whole, whole],
        (flex, u, v, outer, mass, face_perm),
        once,
        in_specs=[HBM] * 6,
        scratch=[
            pltpu.VMEM((size, cases), F32),
            pltpu.VMEM((size, cases), F32),
            pltpu.VMEM((size, cases), BF16),
            pltpu.VMEM((1, size), F32),
            pltpu.VMEM((1, half), jnp.int32),
            pltpu.SemaphoreType.DMA((5,)),
            pltpu.SemaphoreType.DMA((CHUNKS,)),
        ],
    )
    matrix = None
    for step in range(2):
        from_a, from_b = exchange(y_a, y_b)
        if step == 0:
            matrix, order = call(
                prepare_kernel, "prepare", [square, small], (a, onehot), 8 * half**3, scratch=[pltpu.VMEM((half, half), BF16)]
            )
        else:
            early_v, order = call(early_kernel, "early", [whole, small], (onehot, u_a, u_b, early_v), 2 * half * half * 3 * cases)
        q_a, q_b, t_a, t_b, sums = call(
            first_kernel, "first", [face] * 4 + [small], (matrix, y_a, y_b, from_a, from_b, order), 2 * once
        )
        from_a, from_b = exchange(q_a, q_b)
        if step == 0:
            force_m, weight_m, early_u, early_v, rate_own, sums = call(
                ready_kernel,
                "ready",
                [whole] * 4 + [face, small],
                (onehot, force, mass, coarse_rate, u, v, base, sums),
                2 * half * half * 6 * cases,
                in_specs=[VMEM] * 2 + [HBM] * 4 + [VMEM] * 2,
                scratch=[
                    pltpu.VMEM((1, size), F32),
                    pltpu.VMEM((1, size), F32),
                    pltpu.VMEM((size, cases), F32),
                    pltpu.VMEM((size, cases), F32),
                    pltpu.SemaphoreType.DMA((4,)),
                ],
            )
        s_a, s_b, spread = call(
            second_kernel,
            "second",
            [face] * 2 + [((subs, 8, cases), F32)],
            (matrix, q_a, q_b, from_a, from_b, sums),
            2 * once,
        )
        gathered = lax.all_to_all(spread, "sub", 0, 0)
        fields = (gathered, y_a, y_b, q_a, q_b, t_a, t_b, s_a, s_b)
        if step == 0:
            y_a, y_b, u_a, u_b = call(next_kernel, "next", [face] * 4, (matrix,) + fields + (force_m, weight_m), once)

    chips = slices // 2
    rows = half // chips
    two = ((2, half, cases), F32)
    blocks = ((chips, 2, rows, cases), F32)
    groups = [list(range(core, slices, 2)) for core in range(2)]
    light = size * cases * 10

    def swap(value):
        return lax.ppermute(value, "tm", [(t, t ^ 1) for t in range(slices)])

    own, give = call(finish_kernel, "finish", [two, two], (onehot,) + fields + (early_u, early_v), light)
    got = swap(give)
    (parts,) = call(combine_kernel, "combine", [blocks], (own, got, rate_own), light)
    parts = lax.all_to_all(parts, "tm", 0, 0, axis_index_groups=groups)
    (states,) = call(prefix_kernel, "prefix", [blocks], (parts, rate_own), light)
    states = lax.all_to_all(states, "tm", 0, 0, axis_index_groups=groups)
    stay, give = call(end_kernel, "end", [two, two], (states, own, got, rate_own), light)
    end_u, end_v = call(join_kernel, "join", [whole, whole], (stay, swap(give)), light, space=jax.ShapeDtypeStruct)
    return end_u[None, None], end_v[None, None]


def solution(mesh):
    return jax.shard_map(
        on_device,
        mesh=mesh,
        in_specs=(
            P("sub", None, None),
            P("sub", None),
            P("sub", None),
            P("sub", None),
            P("tm", "sub", None, None),
            P("tm", "sub", None, None),
            P("tm", "sub", None, None),
        ),
        out_specs=(P("tm", "sub", None, None), P("tm", "sub", None, None)),
        check_vma=False,
    )
```

```python
import jax
import jax.numpy as jnp
from jax import lax
from jax.experimental import pallas as pl
from jax.experimental.pallas import tpu as pltpu
from jax.sharding import PartitionSpec as P

F32 = jnp.float32
BF16 = jnp.bfloat16
VMEM = pl.BlockSpec(memory_space=pltpu.VMEM)
HBM = pl.BlockSpec(memory_space=pltpu.HBM)
CHUNKS = 8


def call(kernel, name, outs, args, flops=0, in_specs=None, scratch=(), limit=12, space=pltpu.VMEM):
    moved = sum(a.size * a.dtype.itemsize for a in args)
    return pl.pallas_call(
        kernel,
        name=name,
        out_shape=[space(shape, dtype) for shape, dtype in outs],
        in_specs=in_specs or [VMEM] * len(args),
        out_specs=[VMEM] * len(outs),
        scratch_shapes=scratch,
        compiler_params=pltpu.CompilerParams(vmem_limit_bytes=limit * 2**20),
        cost_estimate=pl.CostEstimate(flops=flops, bytes_accessed=moved, transcendentals=0),
    )(*args)


def pair(value):
    high = value.astype(BF16)
    return jnp.concatenate([high, (value - high.astype(F32)).astype(BF16)], axis=1)


def triple(value):
    high = value.astype(BF16)
    rest = value - high.astype(F32)
    middle = rest.astype(BF16)
    low = (rest - middle.astype(F32)).astype(BF16)
    return jnp.concatenate([high, middle, low], axis=1)


def fold(wide):
    return wide[:, :128] + wide[:, 128:256] + wide[:, 256:]


def to_multipliers(onehot, face):
    return fold(jnp.dot(onehot, triple(face), preferred_element_type=F32))


def to_left(onehot, block):
    return fold(lax.dot_general(onehot, triple(block), (((0,), (0,)), ((), ())), preferred_element_type=F32))


def column(row):
    width = row.shape[1]
    pieces = [jnp.transpose(jnp.broadcast_to(row[:, k : k + 128], (128, 128))) for k in range(0, width, 128)]
    return jnp.concatenate(pieces, axis=0)


def add_up(value):
    return jnp.sum(value, axis=0, keepdims=True)


def is_even():
    return lax.rem(lax.axis_index("sub"), 2) == 0


def by_pairs(left, right):
    even = is_even()
    return jnp.where(even, left, right), jnp.where(even, right, left)


def by_sides(face_a, face_b):
    even = is_even()
    return jnp.where(even, face_a, face_b), jnp.where(even, face_b, face_a)


def sides(half, step):
    odd = lax.rem(lax.axis_index("sub"), 2)

    def left(offset, count):
        return pl.ds(pl.multiple_of(odd * half + offset, step), count)

    def right(offset, count):
        return pl.ds(pl.multiple_of((1 - odd) * half + offset, step), count)

    return left, right


def start_kernel(
    a_in, u_in, v_in, load_in, mass_in, perm_in, a, onehot, y_a, y_b, base, force, u, v, load, mass, perm, fields_sem, a_sem
):
    size = a.shape[0]
    half, rows = size // 2, size // CHUNKS
    small = [
        pltpu.make_async_copy(source, target, fields_sem.at[k])
        for k, (source, target) in enumerate(
            [(perm_in, perm), (mass_in, mass), (u_in, u), (v_in, v), (load_in, load)]
        )
    ]
    big = [
        pltpu.make_async_copy(a_in.at[pl.ds(k * rows, rows)], a.at[pl.ds(k * rows, rows)], a_sem.at[k])
        for k in range(CHUNKS)
    ]
    for copy in small:
        copy.start()
    small[0].wait()
    onehot[...] = (lax.broadcasted_iota(jnp.int32, (half, half), 0) == perm[...]).astype(F32).astype(BF16)
    for copy in small[1:]:
        copy.wait()
    for copy in big:
        copy.start()
    weight = 2.0 * column(mass[...])
    outer = load[...].astype(F32)
    rhs = (outer + weight * (u[...] + v[...])).astype(BF16)
    before = 2.0 * u[...] + v[...]
    base[...] = before
    force[...] = outer - weight * before
    faces = []
    for first in (0, CHUNKS // 2):
        parts = []
        for k in range(first, first + CHUNKS // 2):
            big[k].wait()
            parts.append(jnp.dot(a[k * rows : (k + 1) * rows], rhs, preferred_element_type=F32))
        faces.append(jnp.concatenate(parts, axis=0))
        if first == 0:
            faces[0] = to_multipliers(onehot[...], faces[0])
    y_a[...], y_b[...] = by_pairs(*faces)


def prepare_kernel(a, onehot, b, order, turned):
    order[...] = jnp.zeros(order.shape, F32)
    size = a.shape[0]
    half, rows = size // 2, size // 4
    left, right = sides(half, rows)
    hot = onehot[...]
    for k in range(4):
        here = slice(k * rows, (k + 1) * rows)
        block = lax.dot_general(a[here, :half], hot, (((1,), (1,)), ((), ())), preferred_element_type=F32).astype(BF16)
        if k < 2:
            turned[here] = block
        else:
            down = right(k * rows - half, rows)
            b[down, left(0, half)] = block
            b[down, right(0, half)] = a[here, half:]
    for k in range(4):
        here = slice(k * rows, (k + 1) * rows)
        if k < 2:
            block, across = turned[:, here], left(k * rows, rows)
        else:
            block, across = a[:half, here], right(k * rows - half, rows)
        b[left(0, half), across] = jnp.dot(hot, block, preferred_element_type=F32).astype(BF16)


def ready_kernel(onehot, force, mass_in, sums_in, force_m, weight_m, sums, mass, sem):
    copy = pltpu.make_async_copy(mass_in, mass, sem)
    copy.start()
    sums[...] = sums_in[...]
    half = onehot.shape[0]
    copy.wait()
    weight = 6.0 * column(mass[...])
    lane = lax.broadcasted_iota(jnp.int32, (half, 128), 1)
    three = triple(weight[:half])
    packed = jnp.where(
        lane == 0, three[:, :128].astype(F32), jnp.where(lane == 1, three[:, 128:256].astype(F32), three[:, 256:].astype(F32))
    )
    both = jnp.concatenate([triple(force[:half]), jnp.where(lane < 3, packed, 0.0).astype(BF16)], axis=1)
    moved = jnp.dot(onehot[...], both, preferred_element_type=F32)
    force_m[:half], force_m[half:] = by_pairs(fold(moved[:, :384]), force[half:])
    left = jnp.broadcast_to(jnp.sum(moved[:, 384:], axis=1, keepdims=True), (half, 128))
    weight_m[:half], weight_m[half:] = by_pairs(left, weight[half:])


def jump(f_a, f_b, from_a, from_b):
    sub = lax.axis_index("sub")
    alone = jnp.logical_or(sub == 0, sub == lax.axis_size("sub") - 1)
    return jnp.where(alone, 0.0, f_a[...] - from_a[...]), f_b[...] - from_b[...]


def first_kernel(b, y_a, y_b, from_a, from_b, order, q_a, q_b, t_a, t_b, sums):
    half = y_a.shape[0]
    r_a, r_b = jump(y_a, y_b, from_a, from_b)
    wide = jnp.dot(b[...], jnp.concatenate([pair(r_a), pair(r_b)], axis=0), preferred_element_type=F32)
    q = wide[:, :128]
    t = q + wide[:, 128:]
    q_a[...], q_b[...] = q[:half], q[half:]
    t_a[...], t_b[...] = t[:half], t[half:]
    rr = 0.5 * (add_up(r_a * r_a) + add_up(r_b * r_b))
    pw = add_up(r_a * q[:half]) + add_up(r_b * q[half:])
    sums[...] = jnp.concatenate([rr, pw, order[2:]], axis=0)


def second_kernel(b, q_a, q_b, from_a, from_b, sums, s_a, s_b, spread):
    half = q_a.shape[0]
    w_a, w_b = jump(q_a, q_b, from_a, from_b)
    wide = jnp.dot(b[...], jnp.concatenate([pair(w_a), pair(w_b)], axis=0), preferred_element_type=F32)
    s = wide[:, :128] + wide[:, 128:]
    s_a[...], s_b[...] = s[:half], s[half:]
    ww = 0.5 * (add_up(w_a * w_a) + add_up(w_b * w_b))
    wfw = add_up(w_a * s[:half]) + add_up(w_b * s[half:])
    own = jnp.concatenate([sums[:2], ww, wfw, jnp.zeros((4, 128), F32)], axis=0)
    spread[...] = jnp.broadcast_to(own[None], spread.shape)


def corrected(gathered, y_a, y_b, q_a, q_b, t_a, t_b, s_a, s_b):
    total = jnp.sum(gathered[...], axis=0)
    rr, pw, ww, wfw = total[0:1], total[1:2], total[2:3], total[3:4]
    alpha = rr / pw
    ratio = ww / pw
    later = (alpha * alpha * ww - rr) / (alpha * alpha * (wfw - ww * ratio))
    gain = alpha * later

    def face(y, q, t, s):
        return y[...] - alpha * q[...] - gain * (ratio * t[...] - s[...])

    return face(y_a, q_a, t_a, s_a), face(y_b, q_b, t_b, s_b)


def next_kernel(b, gathered, y_a, y_b, q_a, q_b, t_a, t_b, s_a, s_b, force_m, weight_m, z_a, z_b, u_a, u_b):
    half = y_a.shape[0]
    new_a, new_b = corrected(gathered, y_a, y_b, q_a, q_b, t_a, t_b, s_a, s_b)
    u_a[...], u_b[...] = new_a, new_b
    rhs = (force_m[...] + weight_m[...] * jnp.concatenate([new_a, new_b], axis=0)).astype(BF16)
    y = jnp.dot(b[...], rhs, preferred_element_type=F32)
    z_a[...], z_b[...] = y[:half], y[half:]


def coarse(rate):
    scale = 1.0 / (1.0 + rate)
    return (1.0 - rate) * scale, 2.0 * scale, -2.0 * rate * scale


def early_kernel(onehot, u_a, u_b, base, rate_in, u_in, v_in, early_u, early_v, rate_own, order, rate, u, v, sem):
    copies = [
        pltpu.make_async_copy(source, target, sem.at[k]) for k, (source, target) in enumerate([(rate_in, rate), (u_in, u), (v_in, v)])
    ]
    for copy in copies:
        copy.start()
    order[...] = jnp.zeros(order.shape, F32)
    half = u_a.shape[0]
    left, right = by_sides(u_a[...], u_b[...])
    later = jnp.concatenate([to_left(onehot[...], left), right], axis=0)
    for copy in copies:
        copy.wait()
    tm = lax.axis_index("tm")
    rates = column(rate[...])
    rate_own[...] = jnp.where(tm % 2 == 0, rates[:half], rates[half:])
    same, up, down = coarse(rates)
    early_u[...] = -jnp.where(tm == 0, 0.0, same * u[...] + up * v[...])
    early_v[...] = base[...] - 4.0 * later - jnp.where(tm == 0, 0.0, down * u[...] + same * v[...])


def finish_kernel(onehot, gathered, y_a, y_b, q_a, q_b, t_a, t_b, s_a, s_b, early_u, early_v, own, give):
    even = lax.axis_index("tm") % 2 == 0
    half = y_a.shape[0]
    left, right = by_sides(*corrected(gathered, y_a, y_b, q_a, q_b, t_a, t_b, s_a, s_b))
    left = to_left(onehot[...], left)
    for k, (early, factor) in enumerate([(early_u, 1.0), (early_v, 2.0)]):
        top = factor * left + early[:half]
        bottom = factor * right + early[half:]
        own[k] = jnp.where(even, top, bottom)
        give[k] = jnp.where(even, bottom, top)


def step_on(rate, state_u, state_v):
    same, up, down = coarse(rate)
    return same * state_u + up * state_v, down * state_u + same * state_v


def both_slices(own, got):
    even = lax.axis_index("tm") % 2 == 0
    return [jnp.where(even, own[k], got[k]) for k in range(2)], [jnp.where(even, got[k], own[k]) for k in range(2)]


def combine_kernel(own, got, rate_own, blocks):
    rows = blocks.shape[2]
    first, second = both_slices(own, got)
    moved = step_on(rate_own[...], *first)
    for k in range(2):
        both = second[k] + moved[k]
        for place in range(blocks.shape[0]):
            blocks[place, k] = both[place * rows : (place + 1) * rows]


def prefix_kernel(blocks, rate_own, states):
    rows = blocks.shape[2]
    chip = lax.axis_index("tm") // 2
    rate = rate_own[pl.ds(pl.multiple_of(chip * rows, rows), rows)]
    states[0] = jnp.zeros(states.shape[1:], F32)
    state = [blocks[0, k] for k in range(2)]
    for place in range(1, blocks.shape[0]):
        for k in range(2):
            states[place, k] = state[k]
        if place + 1 < blocks.shape[0]:
            moved = step_on(rate, *step_on(rate, *state))
            state = [blocks[place, k] + moved[k] for k in range(2)]


def end_kernel(states, own, got, rate_own, stay, give):
    even = lax.axis_index("tm") % 2 == 0
    first, second = both_slices(own, got)
    rate = rate_own[...]
    entering = [jnp.concatenate([states[place, k] for place in range(states.shape[0])], axis=0) for k in range(2)]
    moved = step_on(rate, *entering)
    first = [first[k] + moved[k] for k in range(2)]
    moved = step_on(rate, *first)
    second = [second[k] + moved[k] for k in range(2)]
    for k in range(2):
        stay[k] = jnp.where(even, first[k], second[k])
        give[k] = jnp.where(even, second[k], first[k])


def join_kernel(stay, got, end_u, end_v):
    even = lax.axis_index("tm") % 2 == 0
    half = stay.shape[1]
    for k, out in enumerate([end_u, end_v]):
        out[:half] = jnp.where(even, stay[k], got[k])
        out[half:] = jnp.where(even, got[k], stay[k])


def on_device(flex, mass, coarse_rate, face_perm, start_u, start_v, load):
    size, cases = start_u.shape[2:]
    half = size // 2
    subs, slices = lax.axis_size("sub"), lax.axis_size("tm")
    flex, mass, coarse_rate, face_perm, u, v, outer = [
        pltpu.with_memory_space_constraint(value, pltpu.HBM)
        for value in (flex[0], mass, coarse_rate, face_perm, start_u[0, 0], start_v[0, 0], load[0, 0])
    ]
    pairs = [[p for s in range(k, subs - 1, 2) for p in ((s, s + 1), (s + 1, s))] for k in (1, 0)]
    face = ((half, cases), F32)
    whole = ((size, cases), F32)
    small = ((8, cases), F32)
    square = ((size, size), BF16)
    once = 2 * size * size * cases

    def exchange(face_a, face_b):
        from_a = lax.ppermute(face_a, "sub", pairs[0])
        return from_a, lax.ppermute(face_b, "sub", pairs[1])

    a, onehot, y_a, y_b, base, force = call(
        start_kernel,
        "start",
        [square, ((half, half), BF16), face, face, whole, whole],
        (flex, u, v, outer, mass, face_perm),
        once,
        in_specs=[HBM] * 6,
        scratch=[
            pltpu.VMEM((size, cases), F32),
            pltpu.VMEM((size, cases), F32),
            pltpu.VMEM((size, cases), BF16),
            pltpu.VMEM((1, size), F32),
            pltpu.VMEM((1, half), jnp.int32),
            pltpu.SemaphoreType.DMA((5,)),
            pltpu.SemaphoreType.DMA((CHUNKS,)),
        ],
    )
    for step in range(2):
        from_a, from_b = exchange(y_a, y_b)
        if step == 0:
            matrix, order = call(
                prepare_kernel, "prepare", [square, small], (a, onehot), 8 * half**3, scratch=[pltpu.VMEM((half, half), BF16)]
            )
        else:
            early_u, early_v, rate_own, order = call(
                early_kernel,
                "early",
                [whole, whole, face, small],
                (onehot, u_a, u_b, base, coarse_rate, u, v),
                2 * half * half * 3 * cases,
                in_specs=[VMEM] * 4 + [HBM] * 3,
                scratch=[
                    pltpu.VMEM((1, size), F32),
                    pltpu.VMEM((size, cases), F32),
                    pltpu.VMEM((size, cases), F32),
                    pltpu.SemaphoreType.DMA((3,)),
                ],
            )
        q_a, q_b, t_a, t_b, sums = call(
            first_kernel, "first", [face] * 4 + [small], (matrix, y_a, y_b, from_a, from_b, order), 2 * once
        )
        from_a, from_b = exchange(q_a, q_b)
        if step == 0:
            force_m, weight_m, sums = call(
                ready_kernel,
                "ready",
                [whole, whole, small],
                (onehot, force, mass, sums),
                2 * half * half * 4 * cases,
                in_specs=[VMEM, VMEM, HBM, VMEM],
                scratch=[pltpu.VMEM((1, size), F32), pltpu.SemaphoreType.DMA(())],
            )
        s_a, s_b, spread = call(
            second_kernel,
            "second",
            [face] * 2 + [((subs, 8, cases), F32)],
            (matrix, q_a, q_b, from_a, from_b, sums),
            2 * once,
        )
        gathered = lax.all_to_all(spread, "sub", 0, 0, axis_index_groups=[list(range(subs))[::-1]])
        fields = (gathered, y_a, y_b, q_a, q_b, t_a, t_b, s_a, s_b)
        if step == 0:
            y_a, y_b, u_a, u_b = call(next_kernel, "next", [face] * 4, (matrix,) + fields + (force_m, weight_m), once)

    chips = slices // 2
    rows = half // chips
    two = ((2, half, cases), F32)
    blocks = ((chips, 2, rows, cases), F32)
    groups = [list(range(core, slices, 2)) for core in range(2)]
    light = size * cases * 10

    def swap(value):
        return lax.ppermute(value, "tm", [(t, t ^ 1) for t in range(slices)])

    own, give = call(finish_kernel, "finish", [two, two], (onehot,) + fields + (early_u, early_v), light)
    got = swap(give)
    (parts,) = call(combine_kernel, "combine", [blocks], (own, got, rate_own), light)
    parts = lax.all_to_all(parts, "tm", 0, 0, axis_index_groups=groups)
    (states,) = call(prefix_kernel, "prefix", [blocks], (parts, rate_own), light)
    states = lax.all_to_all(states, "tm", 0, 0, axis_index_groups=groups)
    stay, give = call(end_kernel, "end", [two, two], (states, own, got, rate_own), light)
    end_u, end_v = call(join_kernel, "join", [whole, whole], (stay, swap(give)), light, space=jax.ShapeDtypeStruct)
    return end_u[None, None], end_v[None, None]


def solution(mesh):
    return jax.shard_map(
        on_device,
        mesh=mesh,
        in_specs=(
            P("sub", None, None),
            P("sub", None),
            P("sub", None),
            P("sub", None),
            P("tm", "sub", None, None),
            P("tm", "sub", None, None),
            P("tm", "sub", None, None),
        ),
        out_specs=(P("tm", "sub", None, None), P("tm", "sub", None, None)),
        check_vma=False,
    )
```

```python
import jax
import jax.numpy as jnp
from jax import lax
from jax.experimental import pallas as pl
from jax.experimental.pallas import tpu as pltpu
from jax.sharding import PartitionSpec as P

F32 = jnp.float32
BF16 = jnp.bfloat16
VMEM = pl.BlockSpec(memory_space=pltpu.VMEM)
HBM = pl.BlockSpec(memory_space=pltpu.HBM)
CHUNKS = 8


def call(kernel, name, outs, args, flops=0, in_specs=None, scratch=(), limit=12, space=pltpu.VMEM):
    moved = sum(a.size * a.dtype.itemsize for a in args)
    return pl.pallas_call(
        kernel,
        name=name,
        out_shape=[space(shape, dtype) for shape, dtype in outs],
        in_specs=in_specs or [VMEM] * len(args),
        out_specs=[VMEM] * len(outs),
        scratch_shapes=scratch,
        compiler_params=pltpu.CompilerParams(vmem_limit_bytes=limit * 2**20),
        cost_estimate=pl.CostEstimate(flops=flops, bytes_accessed=moved, transcendentals=0),
    )(*args)


def pair(value):
    high = value.astype(BF16)
    return jnp.concatenate([high, (value - high.astype(F32)).astype(BF16)], axis=1)


def triple(value):
    high = value.astype(BF16)
    rest = value - high.astype(F32)
    middle = rest.astype(BF16)
    low = (rest - middle.astype(F32)).astype(BF16)
    return jnp.concatenate([high, middle, low], axis=1)


def fold(wide):
    return wide[:, :128] + wide[:, 128:256] + wide[:, 256:]


def to_multipliers(onehot, face):
    return fold(jnp.dot(onehot, triple(face), preferred_element_type=F32))


def to_left(onehot, block):
    return fold(lax.dot_general(onehot, triple(block), (((0,), (0,)), ((), ())), preferred_element_type=F32))


def column(row):
    width = row.shape[1]
    pieces = [jnp.transpose(jnp.broadcast_to(row[:, k : k + 128], (128, 128))) for k in range(0, width, 128)]
    return jnp.concatenate(pieces, axis=0)


def add_up(value):
    return jnp.sum(value, axis=0, keepdims=True)


def is_even():
    return lax.rem(lax.axis_index("sub"), 2) == 0


def by_pairs(left, right):
    even = is_even()
    return jnp.where(even, left, right), jnp.where(even, right, left)


def by_sides(face_a, face_b):
    even = is_even()
    return jnp.where(even, face_a, face_b), jnp.where(even, face_b, face_a)


def sides(half, step):
    odd = lax.rem(lax.axis_index("sub"), 2)

    def left(offset, count):
        return pl.ds(pl.multiple_of(odd * half + offset, step), count)

    def right(offset, count):
        return pl.ds(pl.multiple_of((1 - odd) * half + offset, step), count)

    return left, right


def start_kernel(
    a_in, u_in, v_in, load_in, mass_in, perm_in, a, onehot, y_a, y_b, base, force, u, v, load, mass, perm, fields_sem, a_sem
):
    size = a.shape[0]
    half, rows = size // 2, size // CHUNKS
    small = [
        pltpu.make_async_copy(source, target, fields_sem.at[k])
        for k, (source, target) in enumerate(
            [(perm_in, perm), (mass_in, mass), (u_in, u), (v_in, v), (load_in, load)]
        )
    ]
    big = [
        pltpu.make_async_copy(a_in.at[pl.ds(k * rows, rows)], a.at[pl.ds(k * rows, rows)], a_sem.at[k])
        for k in range(CHUNKS)
    ]
    for copy in small:
        copy.start()
    small[0].wait()
    onehot[...] = (lax.broadcasted_iota(jnp.int32, (half, half), 0) == perm[...]).astype(F32).astype(BF16)
    for copy in small[1:]:
        copy.wait()
    for copy in big:
        copy.start()
    weight = 2.0 * column(mass[...])
    outer = load[...].astype(F32)
    rhs = (outer + weight * (u[...] + v[...])).astype(BF16)
    before = 2.0 * u[...] + v[...]
    base[...] = before
    force[...] = outer - weight * before
    faces = []
    for first in (0, CHUNKS // 2):
        parts = []
        for k in range(first, first + CHUNKS // 2):
            big[k].wait()
            parts.append(jnp.dot(a[k * rows : (k + 1) * rows], rhs, preferred_element_type=F32))
        faces.append(jnp.concatenate(parts, axis=0))
        if first == 0:
            faces[0] = to_multipliers(onehot[...], faces[0])
    y_a[...], y_b[...] = by_pairs(*faces)


def prepare_kernel(a, onehot, b, order, turned):
    order[...] = jnp.zeros(order.shape, F32)
    size = a.shape[0]
    half, rows = size // 2, size // 4
    left, right = sides(half, rows)
    hot = onehot[...]
    for k in range(4):
        here = slice(k * rows, (k + 1) * rows)
        block = lax.dot_general(a[here, :half], hot, (((1,), (1,)), ((), ())), preferred_element_type=F32).astype(BF16)
        if k < 2:
            turned[here] = block
        else:
            down = right(k * rows - half, rows)
            b[down, left(0, half)] = block
            b[down, right(0, half)] = a[here, half:]
    for k in range(4):
        here = slice(k * rows, (k + 1) * rows)
        if k < 2:
            block, across = turned[:, here], left(k * rows, rows)
        else:
            block, across = a[:half, here], right(k * rows - half, rows)
        b[left(0, half), across] = jnp.dot(hot, block, preferred_element_type=F32).astype(BF16)


def ready_kernel(onehot, force, mass_in, sums_in, force_m, weight_m, sums, mass, sem):
    copy = pltpu.make_async_copy(mass_in, mass, sem)
    copy.start()
    sums[...] = sums_in[...]
    half = onehot.shape[0]
    copy.wait()
    weight = 6.0 * column(mass[...])
    lane = lax.broadcasted_iota(jnp.int32, (half, 128), 1)
    three = triple(weight[:half])
    packed = jnp.where(
        lane == 0, three[:, :128].astype(F32), jnp.where(lane == 1, three[:, 128:256].astype(F32), three[:, 256:].astype(F32))
    )
    both = jnp.concatenate([triple(force[:half]), jnp.where(lane < 3, packed, 0.0).astype(BF16)], axis=1)
    moved = jnp.dot(onehot[...], both, preferred_element_type=F32)
    force_m[:half], force_m[half:] = by_pairs(fold(moved[:, :384]), force[half:])
    left = jnp.broadcast_to(jnp.sum(moved[:, 384:], axis=1, keepdims=True), (half, 128))
    weight_m[:half], weight_m[half:] = by_pairs(left, weight[half:])


def jump(f_a, f_b, from_a, from_b):
    sub = lax.axis_index("sub")
    alone = jnp.logical_or(sub == 0, sub == lax.axis_size("sub") - 1)
    return jnp.where(alone, 0.0, f_a[...] - from_a[...]), f_b[...] - from_b[...]


def part_kernel(b, f_b, from_b, part):
    half = f_b.shape[0]
    part[...] = jnp.dot(b[:, half:], pair(f_b[...] - from_b[...]), preferred_element_type=F32)


def first_kernel(b, part, y_a, y_b, from_a, from_b, order, q_a, q_b, t_a, t_b, sums):
    half = y_a.shape[0]
    r_a, r_b = jump(y_a, y_b, from_a, from_b)
    wide = part[...] + jnp.dot(b[:, :half], pair(r_a), preferred_element_type=F32)
    q = wide[:, :128]
    t = q + wide[:, 128:]
    q_a[...], q_b[...] = q[:half], q[half:]
    t_a[...], t_b[...] = t[:half], t[half:]
    rr = 0.5 * (add_up(r_a * r_a) + add_up(r_b * r_b))
    pw = add_up(r_a * q[:half]) + add_up(r_b * q[half:])
    sums[...] = jnp.concatenate([rr, pw, order[2:]], axis=0)


def second_kernel(b, part, q_a, q_b, from_a, from_b, sums, s_a, s_b, spread):
    half = q_a.shape[0]
    w_a, w_b = jump(q_a, q_b, from_a, from_b)
    wide = part[...] + jnp.dot(b[:, :half], pair(w_a), preferred_element_type=F32)
    s = wide[:, :128] + wide[:, 128:]
    s_a[...], s_b[...] = s[:half], s[half:]
    ww = 0.5 * (add_up(w_a * w_a) + add_up(w_b * w_b))
    wfw = add_up(w_a * s[:half]) + add_up(w_b * s[half:])
    own = jnp.concatenate([sums[:2], ww, wfw, jnp.zeros((4, 128), F32)], axis=0)
    spread[...] = jnp.broadcast_to(own[None], spread.shape)


def corrected(gathered, y_a, y_b, q_a, q_b, t_a, t_b, s_a, s_b):
    total = jnp.sum(gathered[...], axis=0)
    rr, pw, ww, wfw = total[0:1], total[1:2], total[2:3], total[3:4]
    alpha = rr / pw
    ratio = ww / pw
    later = (alpha * alpha * ww - rr) / (alpha * alpha * (wfw - ww * ratio))
    gain = alpha * later

    def face(y, q, t, s):
        return y[...] - alpha * q[...] - gain * (ratio * t[...] - s[...])

    return face(y_a, q_a, t_a, s_a), face(y_b, q_b, t_b, s_b)


def next_kernel(b, gathered, y_a, y_b, q_a, q_b, t_a, t_b, s_a, s_b, force_m, weight_m, z_a, z_b, u_a, u_b):
    half = y_a.shape[0]
    new_a, new_b = corrected(gathered, y_a, y_b, q_a, q_b, t_a, t_b, s_a, s_b)
    u_a[...], u_b[...] = new_a, new_b
    rhs = (force_m[...] + weight_m[...] * jnp.concatenate([new_a, new_b], axis=0)).astype(BF16)
    y = jnp.dot(b[...], rhs, preferred_element_type=F32)
    z_a[...], z_b[...] = y[:half], y[half:]


def coarse(rate):
    scale = 1.0 / (1.0 + rate)
    return (1.0 - rate) * scale, 2.0 * scale, -2.0 * rate * scale


def early_kernel(onehot, u_a, u_b, base, rate_in, u_in, v_in, early_u, early_v, rate_own, order, rate, u, v, sem):
    copies = [
        pltpu.make_async_copy(source, target, sem.at[k]) for k, (source, target) in enumerate([(rate_in, rate), (u_in, u), (v_in, v)])
    ]
    for copy in copies:
        copy.start()
    order[...] = jnp.zeros(order.shape, F32)
    half = u_a.shape[0]
    left, right = by_sides(u_a[...], u_b[...])
    later = jnp.concatenate([to_left(onehot[...], left), right], axis=0)
    for copy in copies:
        copy.wait()
    tm = lax.axis_index("tm")
    rates = column(rate[...])
    rate_own[...] = jnp.where(tm % 2 == 0, rates[:half], rates[half:])
    same, up, down = coarse(rates)
    early_u[...] = -jnp.where(tm == 0, 0.0, same * u[...] + up * v[...])
    early_v[...] = base[...] - 4.0 * later - jnp.where(tm == 0, 0.0, down * u[...] + same * v[...])


def finish_kernel(onehot, gathered, y_a, y_b, q_a, q_b, t_a, t_b, s_a, s_b, early_u, early_v, own, give):
    even = lax.axis_index("tm") % 2 == 0
    half = y_a.shape[0]
    left, right = by_sides(*corrected(gathered, y_a, y_b, q_a, q_b, t_a, t_b, s_a, s_b))
    left = to_left(onehot[...], left)
    for k, (early, factor) in enumerate([(early_u, 1.0), (early_v, 2.0)]):
        top = factor * left + early[:half]
        bottom = factor * right + early[half:]
        own[k] = jnp.where(even, top, bottom)
        give[k] = jnp.where(even, bottom, top)


def step_on(rate, state_u, state_v):
    same, up, down = coarse(rate)
    return same * state_u + up * state_v, down * state_u + same * state_v


def both_slices(own, got):
    even = lax.axis_index("tm") % 2 == 0
    return [jnp.where(even, own[k], got[k]) for k in range(2)], [jnp.where(even, got[k], own[k]) for k in range(2)]


def combine_kernel(own, got, rate_own, blocks):
    rows = blocks.shape[2]
    first, second = both_slices(own, got)
    moved = step_on(rate_own[...], *first)
    for k in range(2):
        both = second[k] + moved[k]
        for place in range(blocks.shape[0]):
            blocks[place, k] = both[place * rows : (place + 1) * rows]


def prefix_kernel(blocks, rate_own, states):
    rows = blocks.shape[2]
    chip = lax.axis_index("tm") // 2
    rate = rate_own[pl.ds(pl.multiple_of(chip * rows, rows), rows)]
    states[0] = jnp.zeros(states.shape[1:], F32)
    state = [blocks[0, k] for k in range(2)]
    for place in range(1, blocks.shape[0]):
        for k in range(2):
            states[place, k] = state[k]
        if place + 1 < blocks.shape[0]:
            moved = step_on(rate, *step_on(rate, *state))
            state = [blocks[place, k] + moved[k] for k in range(2)]


def end_kernel(states, own, got, rate_own, stay, give):
    even = lax.axis_index("tm") % 2 == 0
    first, second = both_slices(own, got)
    rate = rate_own[...]
    entering = [jnp.concatenate([states[place, k] for place in range(states.shape[0])], axis=0) for k in range(2)]
    moved = step_on(rate, *entering)
    first = [first[k] + moved[k] for k in range(2)]
    moved = step_on(rate, *first)
    second = [second[k] + moved[k] for k in range(2)]
    for k in range(2):
        stay[k] = jnp.where(even, first[k], second[k])
        give[k] = jnp.where(even, second[k], first[k])


def join_kernel(stay, got, end_u, end_v):
    even = lax.axis_index("tm") % 2 == 0
    half = stay.shape[1]
    for k, out in enumerate([end_u, end_v]):
        out[:half] = jnp.where(even, stay[k], got[k])
        out[half:] = jnp.where(even, got[k], stay[k])


def on_device(flex, mass, coarse_rate, face_perm, start_u, start_v, load):
    size, cases = start_u.shape[2:]
    half = size // 2
    subs, slices = lax.axis_size("sub"), lax.axis_size("tm")
    flex, mass, coarse_rate, face_perm, u, v, outer = [
        pltpu.with_memory_space_constraint(value, pltpu.HBM)
        for value in (flex[0], mass, coarse_rate, face_perm, start_u[0, 0], start_v[0, 0], load[0, 0])
    ]
    pairs = [[p for s in range(k, subs - 1, 2) for p in ((s, s + 1), (s + 1, s))] for k in (1, 0)]
    face = ((half, cases), F32)
    whole = ((size, cases), F32)
    wide = ((size, 2 * cases), F32)
    small = ((8, cases), F32)
    square = ((size, size), BF16)
    once = 2 * size * size * cases

    def exchange(face_a, face_b):
        from_a = lax.ppermute(face_a, "sub", pairs[0])
        return from_a, lax.ppermute(face_b, "sub", pairs[1])

    a, onehot, y_a, y_b, base, force = call(
        start_kernel,
        "start",
        [square, ((half, half), BF16), face, face, whole, whole],
        (flex, u, v, outer, mass, face_perm),
        once,
        in_specs=[HBM] * 6,
        scratch=[
            pltpu.VMEM((size, cases), F32),
            pltpu.VMEM((size, cases), F32),
            pltpu.VMEM((size, cases), BF16),
            pltpu.VMEM((1, size), F32),
            pltpu.VMEM((1, half), jnp.int32),
            pltpu.SemaphoreType.DMA((5,)),
            pltpu.SemaphoreType.DMA((CHUNKS,)),
        ],
    )
    for step in range(2):
        from_a, from_b = exchange(y_a, y_b)
        if step == 0:
            matrix, order = call(
                prepare_kernel, "prepare", [square, small], (a, onehot), 8 * half**3, scratch=[pltpu.VMEM((half, half), BF16)]
            )
        else:
            early_u, early_v, rate_own, order = call(
                early_kernel,
                "early",
                [whole, whole, face, small],
                (onehot, u_a, u_b, base, coarse_rate, u, v),
                2 * half * half * 3 * cases,
                in_specs=[VMEM] * 4 + [HBM] * 3,
                scratch=[
                    pltpu.VMEM((1, size), F32),
                    pltpu.VMEM((size, cases), F32),
                    pltpu.VMEM((size, cases), F32),
                    pltpu.SemaphoreType.DMA((3,)),
                ],
            )
        (part,) = call(part_kernel, "part", [wide], (matrix, y_b, from_b), once)
        q_a, q_b, t_a, t_b, sums = call(
            first_kernel, "first", [face] * 4 + [small], (matrix, part, y_a, y_b, from_a, from_b, order), once
        )
        from_a, from_b = exchange(q_a, q_b)
        if step == 0:
            force_m, weight_m, sums = call(
                ready_kernel,
                "ready",
                [whole, whole, small],
                (onehot, force, mass, sums),
                2 * half * half * 4 * cases,
                in_specs=[VMEM, VMEM, HBM, VMEM],
                scratch=[pltpu.VMEM((1, size), F32), pltpu.SemaphoreType.DMA(())],
            )
        (part,) = call(part_kernel, "part", [wide], (matrix, q_b, from_b), once)
        s_a, s_b, spread = call(
            second_kernel,
            "second",
            [face] * 2 + [((subs, 8, cases), F32)],
            (matrix, part, q_a, q_b, from_a, from_b, sums),
            once,
        )
        gathered = lax.all_to_all(spread, "sub", 0, 0, axis_index_groups=[list(range(subs))[::-1]])
        fields = (gathered, y_a, y_b, q_a, q_b, t_a, t_b, s_a, s_b)
        if step == 0:
            y_a, y_b, u_a, u_b = call(next_kernel, "next", [face] * 4, (matrix,) + fields + (force_m, weight_m), once)

    chips = slices // 2
    rows = half // chips
    two = ((2, half, cases), F32)
    blocks = ((chips, 2, rows, cases), F32)
    groups = [list(range(core, slices, 2)) for core in range(2)]
    light = size * cases * 10

    def swap(value):
        return lax.ppermute(value, "tm", [(t, t ^ 1) for t in range(slices)])

    own, give = call(finish_kernel, "finish", [two, two], (onehot,) + fields + (early_u, early_v), light)
    got = swap(give)
    (parts,) = call(combine_kernel, "combine", [blocks], (own, got, rate_own), light)
    parts = lax.all_to_all(parts, "tm", 0, 0, axis_index_groups=groups)
    (states,) = call(prefix_kernel, "prefix", [blocks], (parts, rate_own), light)
    states = lax.all_to_all(states, "tm", 0, 0, axis_index_groups=groups)
    stay, give = call(end_kernel, "end", [two, two], (states, own, got, rate_own), light)
    end_u, end_v = call(join_kernel, "join", [whole, whole], (stay, swap(give)), light, space=jax.ShapeDtypeStruct)
    return end_u[None, None], end_v[None, None]


def solution(mesh):
    return jax.shard_map(
        on_device,
        mesh=mesh,
        in_specs=(
            P("sub", None, None),
            P("sub", None),
            P("sub", None),
            P("sub", None),
            P("tm", "sub", None, None),
            P("tm", "sub", None, None),
            P("tm", "sub", None, None),
        ),
        out_specs=(P("tm", "sub", None, None), P("tm", "sub", None, None)),
        check_vma=False,
    )
```

```python
import jax
import jax.numpy as jnp
from jax import lax
from jax.experimental import pallas as pl
from jax.experimental.pallas import tpu as pltpu
from jax.sharding import PartitionSpec as P

F32 = jnp.float32
BF16 = jnp.bfloat16
VMEM = pl.BlockSpec(memory_space=pltpu.VMEM)
HBM = pl.BlockSpec(memory_space=pltpu.HBM)
CHUNKS = 8


def call(kernel, name, outs, args, flops=0, moved=None, in_specs=None, scratch=(), limit=12, in_hbm=False, aliases=None):
    moved = moved or sum(a.size * a.dtype.itemsize for a in args)
    return pl.pallas_call(
        kernel,
        name=name,
        out_shape=[(jax.ShapeDtypeStruct if in_hbm else pltpu.VMEM)(shape, dtype) for shape, dtype in outs],
        in_specs=in_specs or [VMEM] * len(args),
        out_specs=[HBM if in_hbm else VMEM] * len(outs),
        scratch_shapes=scratch,
        input_output_aliases=aliases or {},
        compiler_params=pltpu.CompilerParams(vmem_limit_bytes=limit * 2**20),
        cost_estimate=pl.CostEstimate(flops=flops, bytes_accessed=moved, transcendentals=0),
    )(*args)


def pair(value):
    high = value.astype(BF16)
    return jnp.concatenate([high, (value - high.astype(F32)).astype(BF16)], axis=1)


def triple(value):
    high = value.astype(BF16)
    rest = value - high.astype(F32)
    middle = rest.astype(BF16)
    low = (rest - middle.astype(F32)).astype(BF16)
    return jnp.concatenate([high, middle, low], axis=1)


def fold(wide):
    return wide[:, :128] + wide[:, 128:256] + wide[:, 256:]


def to_multipliers(onehot, face):
    return fold(jnp.dot(onehot, triple(face), preferred_element_type=F32))


def to_left(onehot, block):
    return fold(lax.dot_general(onehot, triple(block), (((0,), (0,)), ((), ())), preferred_element_type=F32))


def column(row):
    width = row.shape[1]
    pieces = [jnp.transpose(jnp.broadcast_to(row[:, k : k + 128], (128, 128))) for k in range(0, width, 128)]
    return jnp.concatenate(pieces, axis=0)


def add_up(value):
    return jnp.sum(value, axis=0, keepdims=True)


def is_even():
    return lax.rem(lax.axis_index("sub"), 2) == 0


def by_pairs(left, right):
    even = is_even()
    return jnp.where(even, left, right), jnp.where(even, right, left)


def by_sides(face_a, face_b):
    even = is_even()
    return jnp.where(even, face_a, face_b), jnp.where(even, face_b, face_a)


def sides(half, step):
    odd = lax.rem(lax.axis_index("sub"), 2)

    def left(offset, count):
        return pl.ds(pl.multiple_of(odd * half + offset, step), count)

    def right(offset, count):
        return pl.ds(pl.multiple_of((1 - odd) * half + offset, step), count)

    return left, right


def start_kernel(
    a_in, u_in, v_in, load_in, mass_in, perm_in, a, onehot, y_a, y_b, base, force, u, v, load, mass, perm, fields_sem, a_sem
):
    size = a.shape[0]
    half, rows = size // 2, size // CHUNKS
    small = [
        pltpu.make_async_copy(source, target, fields_sem.at[k])
        for k, (source, target) in enumerate(
            [(perm_in, perm), (mass_in, mass), (u_in, u), (v_in, v), (load_in, load)]
        )
    ]
    big = [
        pltpu.make_async_copy(a_in.at[pl.ds(k * rows, rows)], a.at[pl.ds(k * rows, rows)], a_sem.at[k])
        for k in range(CHUNKS)
    ]
    for copy in small + big[:2]:
        copy.start()
    small[0].wait()
    onehot[...] = (lax.broadcasted_iota(jnp.int32, (half, half), 0) == perm[...]).astype(F32).astype(BF16)
    for copy in small[1:]:
        copy.wait()
    for copy in big[2:]:
        copy.start()
    weight = 2.0 * column(mass[...])
    outer = load[...].astype(F32)
    rhs = (outer + weight * (u[...] + v[...])).astype(BF16)
    before = 2.0 * u[...] + v[...]
    base[...] = before
    force[...] = outer - weight * before
    faces = []
    for first in (0, CHUNKS // 2):
        parts = []
        for k in range(first, first + CHUNKS // 2):
            big[k].wait()
            parts.append(jnp.dot(a[k * rows : (k + 1) * rows], rhs, preferred_element_type=F32))
        faces.append(jnp.concatenate(parts, axis=0))
        if first == 0:
            faces[0] = to_multipliers(onehot[...], faces[0])
    y_a[...], y_b[...] = by_pairs(*faces)


def prepare_kernel(a, onehot, b, order, turned):
    order[...] = jnp.zeros(order.shape, F32)
    size = a.shape[0]
    half, rows = size // 2, size // 4
    left, right = sides(half, rows)
    hot = onehot[...]
    for k in range(4):
        here = slice(k * rows, (k + 1) * rows)
        block = lax.dot_general(a[here, :half], hot, (((1,), (1,)), ((), ())), preferred_element_type=F32).astype(BF16)
        if k < 2:
            turned[here] = block
        else:
            down = right(k * rows - half, rows)
            b[down, left(0, half)] = block
            b[down, right(0, half)] = a[here, half:]
    for k in range(4):
        here = slice(k * rows, (k + 1) * rows)
        if k < 2:
            block, across = turned[:, here], left(k * rows, rows)
        else:
            block, across = a[:half, here], right(k * rows - half, rows)
        b[left(0, half), across] = jnp.dot(hot, block, preferred_element_type=F32).astype(BF16)


def ready_kernel(onehot, force, mass_in, sums_in, force_m, weight_m, sums, mass, sem):
    copy = pltpu.make_async_copy(mass_in, mass, sem)
    copy.start()
    sums[...] = sums_in[...]
    half = onehot.shape[0]
    copy.wait()
    weight = 6.0 * column(mass[...])
    lane = lax.broadcasted_iota(jnp.int32, (half, 128), 1)
    three = triple(weight[:half])
    packed = jnp.where(
        lane == 0, three[:, :128].astype(F32), jnp.where(lane == 1, three[:, 128:256].astype(F32), three[:, 256:].astype(F32))
    )
    both = jnp.concatenate([triple(force[:half]), jnp.where(lane < 3, packed, 0.0).astype(BF16)], axis=1)
    moved = jnp.dot(onehot[...], both, preferred_element_type=F32)
    force_m[:half], force_m[half:] = by_pairs(fold(moved[:, :384]), force[half:])
    left = jnp.broadcast_to(jnp.sum(moved[:, 384:], axis=1, keepdims=True), (half, 128))
    weight_m[:half], weight_m[half:] = by_pairs(left, weight[half:])


def jump(f_a, f_b, from_a, from_b):
    sub = lax.axis_index("sub")
    alone = jnp.logical_or(sub == 0, sub == lax.axis_size("sub") - 1)
    return jnp.where(alone, 0.0, f_a[...] - from_a[...]), f_b[...] - from_b[...]


def part_kernel(b, f_b, from_b, part):
    half = f_b.shape[0]
    part[...] = jnp.dot(b[:, half:], pair(f_b[...] - from_b[...]), preferred_element_type=F32)


def first_kernel(b, part, y_a, y_b, from_a, from_b, order, q_a, q_b, t_a, t_b, sums):
    half = y_a.shape[0]
    r_a, r_b = jump(y_a, y_b, from_a, from_b)
    wide = part[...] + jnp.dot(b[:, :half], pair(r_a), preferred_element_type=F32)
    q = wide[:, :128]
    t = q + wide[:, 128:]
    q_a[...], q_b[...] = q[:half], q[half:]
    t_a[...], t_b[...] = t[:half], t[half:]
    rr = 0.5 * (add_up(r_a * r_a) + add_up(r_b * r_b))
    pw = add_up(r_a * q[:half]) + add_up(r_b * q[half:])
    sums[...] = jnp.concatenate([rr, pw, order[2:]], axis=0)


def second_kernel(b, part, q_a, q_b, from_a, from_b, sums, s_a, s_b, spread):
    half = q_a.shape[0]
    w_a, w_b = jump(q_a, q_b, from_a, from_b)
    wide = part[...] + jnp.dot(b[:, :half], pair(w_a), preferred_element_type=F32)
    s = wide[:, :128] + wide[:, 128:]
    s_a[...], s_b[...] = s[:half], s[half:]
    ww = 0.5 * (add_up(w_a * w_a) + add_up(w_b * w_b))
    wfw = add_up(w_a * s[:half]) + add_up(w_b * s[half:])
    own = jnp.concatenate([sums[:2], ww, wfw], axis=0)
    spread[...] = jnp.broadcast_to(own[None], spread.shape)


def corrected(gathered, y_a, y_b, q_a, q_b, t_a, t_b, s_a, s_b):
    total = jnp.sum(gathered[...], axis=0)
    rr, pw, ww, wfw = total[0:1], total[1:2], total[2:3], total[3:4]
    alpha = rr / pw
    ratio = ww / pw
    later = (alpha * alpha * ww - rr) / (alpha * alpha * (wfw - ww * ratio))
    gain = alpha * later

    def face(y, q, t, s):
        return y[...] - alpha * q[...] - gain * (ratio * t[...] - s[...])

    return face(y_a, q_a, t_a, s_a), face(y_b, q_b, t_b, s_b)


def next_kernel(b, gathered, y_a, y_b, q_a, q_b, t_a, t_b, s_a, s_b, force_m, weight_m, z_a, z_b, u_a, u_b):
    half = y_a.shape[0]
    new_a, new_b = corrected(gathered, y_a, y_b, q_a, q_b, t_a, t_b, s_a, s_b)
    u_a[...], u_b[...] = new_a, new_b
    rhs = (force_m[...] + weight_m[...] * jnp.concatenate([new_a, new_b], axis=0)).astype(BF16)
    y = jnp.dot(b[...], rhs, preferred_element_type=F32)
    z_a[...], z_b[...] = y[:half], y[half:]


def coarse(rate):
    scale = 1.0 / (1.0 + rate)
    return (1.0 - rate) * scale, 2.0 * scale, -2.0 * rate * scale


def early_kernel(onehot, u_a, u_b, base, rate_in, u_in, v_in, early_u, early_v, rate_own, order, rate, u, v, sem):
    copies = [
        pltpu.make_async_copy(source, target, sem.at[k]) for k, (source, target) in enumerate([(rate_in, rate), (u_in, u), (v_in, v)])
    ]
    for copy in copies:
        copy.start()
    order[...] = jnp.zeros(order.shape, F32)
    half = u_a.shape[0]
    left, right = by_sides(u_a[...], u_b[...])
    later = jnp.concatenate([to_left(onehot[...], left), right], axis=0)
    for copy in copies:
        copy.wait()
    tm = lax.axis_index("tm")
    rates = column(rate[...])
    rate_own[...] = jnp.where(tm % 2 == 0, rates[:half], rates[half:])
    same, up, down = coarse(rates)
    early_u[...] = -jnp.where(tm == 0, 0.0, same * u[...] + up * v[...])
    early_v[...] = base[...] - 4.0 * later - jnp.where(tm == 0, 0.0, down * u[...] + same * v[...])


def finish_kernel(onehot, gathered, y_a, y_b, q_a, q_b, t_a, t_b, s_a, s_b, early_u, early_v, own, give):
    even = lax.axis_index("tm") % 2 == 0
    half = y_a.shape[0]
    left, right = by_sides(*corrected(gathered, y_a, y_b, q_a, q_b, t_a, t_b, s_a, s_b))
    left = to_left(onehot[...], left)
    for k, (early, factor) in enumerate([(early_u, 1.0), (early_v, 2.0)]):
        top = factor * left + early[:half]
        bottom = factor * right + early[half:]
        own[k] = jnp.where(even, top, bottom)
        give[k] = jnp.where(even, bottom, top)


def step_on(rate, state_u, state_v):
    same, up, down = coarse(rate)
    return same * state_u + up * state_v, down * state_u + same * state_v


def both_slices(own, got):
    even = lax.axis_index("tm") % 2 == 0
    return [jnp.where(even, own[k], got[k]) for k in range(2)], [jnp.where(even, got[k], own[k]) for k in range(2)]


def combine_kernel(own, got, rate_own, blocks):
    rows = blocks.shape[2]
    first, second = both_slices(own, got)
    moved = step_on(rate_own[...], *first)
    for k in range(2):
        both = second[k] + moved[k]
        for place in range(blocks.shape[0]):
            blocks[place, k] = both[place * rows : (place + 1) * rows]


def prefix_kernel(blocks, rate_own, states):
    rows = blocks.shape[2]
    chip = lax.axis_index("tm") // 2
    rate = rate_own[pl.ds(pl.multiple_of(chip * rows, rows), rows)]
    states[0] = jnp.zeros(states.shape[1:], F32)
    state = [blocks[0, k] for k in range(2)]
    for place in range(1, blocks.shape[0]):
        for k in range(2):
            states[place, k] = state[k]
        if place + 1 < blocks.shape[0]:
            moved = step_on(rate, *step_on(rate, *state))
            state = [blocks[place, k] + moved[k] for k in range(2)]


def end_kernel(states, own, got, rate_own, stay, give):
    even = lax.axis_index("tm") % 2 == 0
    first, second = both_slices(own, got)
    rate = rate_own[...]
    entering = [jnp.concatenate([states[place, k] for place in range(states.shape[0])], axis=0) for k in range(2)]
    moved = step_on(rate, *entering)
    first = [first[k] + moved[k] for k in range(2)]
    moved = step_on(rate, *first)
    second = [second[k] + moved[k] for k in range(2)]
    for k in range(2):
        stay[k] = jnp.where(even, first[k], second[k])
        give[k] = jnp.where(even, second[k], first[k])


def copy_half(source, outs, start, sem):
    half = source.shape[1]
    place = pl.ds(pl.multiple_of(start, half), half)
    copies = [pltpu.make_async_copy(source.at[k], out.at[place], sem.at[k]) for k, out in enumerate(outs)]
    for copy in copies:
        copy.start()
    for copy in copies:
        copy.wait()


def keep_kernel(stay, end_u, end_v, sem):
    core = lax.rem(lax.axis_index("tm"), 2)
    copy_half(stay, [end_u, end_v], core * stay.shape[1], sem)


def join_kernel(got, in_u, in_v, end_u, end_v, sem):
    core = lax.rem(lax.axis_index("tm"), 2)
    copy_half(got, [end_u, end_v], (1 - core) * got.shape[1], sem)


def on_device(flex, mass, coarse_rate, face_perm, start_u, start_v, load):
    size, cases = start_u.shape[2:]
    half = size // 2
    subs, slices = lax.axis_size("sub"), lax.axis_size("tm")
    flex, mass, coarse_rate, face_perm, u, v, outer = [
        pltpu.with_memory_space_constraint(value, pltpu.HBM)
        for value in (flex[0], mass, coarse_rate, face_perm, start_u[0, 0], start_v[0, 0], load[0, 0])
    ]
    pairs = [[p for s in range(k, subs - 1, 2) for p in ((s, s + 1), (s + 1, s))] for k in (1, 0)]
    face = ((half, cases), F32)
    whole = ((size, cases), F32)
    wide = ((size, 2 * cases), F32)
    small = ((8, cases), F32)
    square = ((size, size), BF16)
    once = 2 * size * size * cases

    def exchange(face_a, face_b):
        from_a = lax.ppermute(face_a, "sub", pairs[0])
        return from_a, lax.ppermute(face_b, "sub", pairs[1])

    a, onehot, y_a, y_b, base, force = call(
        start_kernel,
        "start",
        [square, ((half, half), BF16), face, face, whole, whole],
        (flex, u, v, outer, mass, face_perm),
        once,
        in_specs=[HBM] * 6,
        scratch=[
            pltpu.VMEM((size, cases), F32),
            pltpu.VMEM((size, cases), F32),
            pltpu.VMEM((size, cases), BF16),
            pltpu.VMEM((1, size), F32),
            pltpu.VMEM((1, half), jnp.int32),
            pltpu.SemaphoreType.DMA((5,)),
            pltpu.SemaphoreType.DMA((CHUNKS,)),
        ],
    )
    for step in range(2):
        from_a, from_b = exchange(y_a, y_b)
        if step == 0:
            matrix, order = call(
                prepare_kernel, "prepare", [square, small], (a, onehot), once, moved=half * cases, scratch=[pltpu.VMEM((half, half), BF16)]
            )
        else:
            early_u, early_v, rate_own, order = call(
                early_kernel,
                "early",
                [whole, whole, face, small],
                (onehot, u_a, u_b, base, coarse_rate, u, v),
                2 * half * half * 3 * cases,
                in_specs=[VMEM] * 4 + [HBM] * 3,
                scratch=[
                    pltpu.VMEM((1, size), F32),
                    pltpu.VMEM((size, cases), F32),
                    pltpu.VMEM((size, cases), F32),
                    pltpu.SemaphoreType.DMA((3,)),
                ],
            )
        (part,) = call(part_kernel, "part", [wide], (matrix, y_b, from_b), once)
        q_a, q_b, t_a, t_b, sums = call(
            first_kernel, "first", [face] * 4 + [small], (matrix, part, y_a, y_b, from_a, from_b, order), once
        )
        from_a, from_b = exchange(q_a, q_b)
        if step == 0:
            force_m, weight_m, sums = call(
                ready_kernel,
                "ready",
                [whole, whole, small],
                (onehot, force, mass, sums),
                2 * half * half * 4 * cases,
                in_specs=[VMEM, VMEM, HBM, VMEM],
                scratch=[pltpu.VMEM((1, size), F32), pltpu.SemaphoreType.DMA(())],
            )
        (part,) = call(part_kernel, "part", [wide], (matrix, q_b, from_b), once)
        s_a, s_b, spread = call(
            second_kernel,
            "second",
            [face] * 2 + [((subs, 4, cases), F32)],
            (matrix, part, q_a, q_b, from_a, from_b, sums),
            once,
        )
        gathered = lax.all_to_all(spread, "sub", 0, 0, axis_index_groups=[list(range(subs))[::-1]])
        fields = (gathered, y_a, y_b, q_a, q_b, t_a, t_b, s_a, s_b)
        if step == 0:
            y_a, y_b, u_a, u_b = call(next_kernel, "next", [face] * 4, (matrix,) + fields + (force_m, weight_m), once)

    chips = slices // 2
    rows = half // chips
    two = ((2, half, cases), F32)
    blocks = ((chips, 2, rows, cases), F32)
    groups = [list(range(core, slices, 2)) for core in range(2)]
    light = size * cases * 10

    def swap(value):
        return lax.ppermute(value, "tm", [(t, t ^ 1) for t in range(slices)])

    own, give = call(finish_kernel, "finish", [two, two], (onehot,) + fields + (early_u, early_v), light)
    got = swap(give)
    (parts,) = call(combine_kernel, "combine", [blocks], (own, got, rate_own), light)
    parts = lax.all_to_all(parts, "tm", 0, 0, axis_index_groups=groups)
    (states,) = call(prefix_kernel, "prefix", [blocks], (parts, rate_own), light)
    states = lax.all_to_all(states, "tm", 0, 0, axis_index_groups=groups)
    stay, give = call(end_kernel, "end", [two, two], (states, own, got, rate_own), light)
    got = swap(give)
    ends = dict(in_hbm=True, scratch=[pltpu.SemaphoreType.DMA((2,))])
    end_u, end_v = call(keep_kernel, "keep", [whole] * 2, (stay,), **ends)
    end_u, end_v = call(
        join_kernel, "join", [whole] * 2, (got, end_u, end_v), in_specs=[VMEM, HBM, HBM], aliases={1: 0, 2: 1}, **ends
    )
    return end_u[None, None], end_v[None, None]


def solution(mesh):
    return jax.shard_map(
        on_device,
        mesh=mesh,
        in_specs=(
            P("sub", None, None),
            P("sub", None),
            P("sub", None),
            P("sub", None),
            P("tm", "sub", None, None),
            P("tm", "sub", None, None),
            P("tm", "sub", None, None),
        ),
        out_specs=(P("tm", "sub", None, None), P("tm", "sub", None, None)),
        check_vma=False,
    )
```

```python
import jax
import jax.numpy as jnp
from jax import lax
from jax.experimental import pallas as pl
from jax.experimental.pallas import tpu as pltpu
from jax.sharding import PartitionSpec as P

F32 = jnp.float32
BF16 = jnp.bfloat16
VMEM = pl.BlockSpec(memory_space=pltpu.VMEM)
HBM = pl.BlockSpec(memory_space=pltpu.HBM)
CHUNKS = 8


def call(kernel, name, outs, args, flops=0, moved=None, in_specs=None, scratch=(), limit=12, in_hbm=False, aliases=None):
    moved = moved or sum(a.size * a.dtype.itemsize for a in args)
    return pl.pallas_call(
        kernel,
        name=name,
        out_shape=[(jax.ShapeDtypeStruct if in_hbm else pltpu.VMEM)(shape, dtype) for shape, dtype in outs],
        in_specs=in_specs or [VMEM] * len(args),
        out_specs=[HBM if in_hbm else VMEM] * len(outs),
        scratch_shapes=scratch,
        input_output_aliases=aliases or {},
        compiler_params=pltpu.CompilerParams(vmem_limit_bytes=limit * 2**20),
        cost_estimate=pl.CostEstimate(flops=flops, bytes_accessed=moved, transcendentals=0),
    )(*args)


def pair(value):
    high = value.astype(BF16)
    return jnp.concatenate([high, (value - high.astype(F32)).astype(BF16)], axis=1)


def triple(value):
    high = value.astype(BF16)
    rest = value - high.astype(F32)
    middle = rest.astype(BF16)
    low = (rest - middle.astype(F32)).astype(BF16)
    return jnp.concatenate([high, middle, low], axis=1)


def fold(wide):
    return wide[:, :128] + wide[:, 128:256] + wide[:, 256:]


def to_multipliers(onehot, face):
    return fold(jnp.dot(onehot, triple(face), preferred_element_type=F32))


def to_left(onehot, block):
    return fold(lax.dot_general(onehot, triple(block), (((0,), (0,)), ((), ())), preferred_element_type=F32))


def column(row):
    width = row.shape[1]
    pieces = [jnp.transpose(jnp.broadcast_to(row[:, k : k + 128], (128, 128))) for k in range(0, width, 128)]
    return jnp.concatenate(pieces, axis=0)


def add_up(value):
    return jnp.sum(value, axis=0, keepdims=True)


def is_even():
    return lax.rem(lax.axis_index("sub"), 2) == 0


def by_pairs(left, right):
    even = is_even()
    return jnp.where(even, left, right), jnp.where(even, right, left)


def by_sides(face_a, face_b):
    even = is_even()
    return jnp.where(even, face_a, face_b), jnp.where(even, face_b, face_a)


def sides(half, step):
    odd = lax.rem(lax.axis_index("sub"), 2)

    def left(offset, count):
        return pl.ds(pl.multiple_of(odd * half + offset, step), count)

    def right(offset, count):
        return pl.ds(pl.multiple_of((1 - odd) * half + offset, step), count)

    return left, right


def start_kernel(
    a_in, u_in, v_in, load_in, mass_in, perm_in, a, onehot, y_a, y_b, base, force, u, v, load, mass, perm, fields_sem, a_sem
):
    size = a.shape[0]
    half, rows = size // 2, size // CHUNKS
    small = [
        pltpu.make_async_copy(source, target, fields_sem.at[k])
        for k, (source, target) in enumerate(
            [(perm_in, perm), (mass_in, mass), (u_in, u), (v_in, v), (load_in, load)]
        )
    ]
    big = [
        pltpu.make_async_copy(a_in.at[pl.ds(k * rows, rows)], a.at[pl.ds(k * rows, rows)], a_sem.at[k])
        for k in range(CHUNKS)
    ]
    for copy in small + big[:2]:
        copy.start()
    small[0].wait()
    onehot[...] = (lax.broadcasted_iota(jnp.int32, (half, half), 0) == perm[...]).astype(F32).astype(BF16)
    for copy in small[1:]:
        copy.wait()
    for copy in big[2:]:
        copy.start()
    weight = 2.0 * column(mass[...])
    outer = load[...].astype(F32)
    rhs = (outer + weight * (u[...] + v[...])).astype(BF16)
    before = 2.0 * u[...] + v[...]
    base[...] = before
    force[...] = outer - weight * before
    faces = []
    for first in (0, CHUNKS // 2):
        parts = []
        for k in range(first, first + CHUNKS // 2):
            big[k].wait()
            parts.append(jnp.dot(a[k * rows : (k + 1) * rows], rhs, preferred_element_type=F32))
        faces.append(jnp.concatenate(parts, axis=0))
        if first == 0:
            faces[0] = to_multipliers(onehot[...], faces[0])
    y_a[...], y_b[...] = by_pairs(*faces)


def prepare_kernel(a, onehot, b, order, turned):
    order[...] = jnp.zeros(order.shape, F32)
    size = a.shape[0]
    half, rows = size // 2, size // 4
    left, right = sides(half, rows)
    hot = onehot[...]
    for k in range(4):
        here = slice(k * rows, (k + 1) * rows)
        block = lax.dot_general(a[here, :half], hot, (((1,), (1,)), ((), ())), preferred_element_type=F32).astype(BF16)
        if k < 2:
            turned[here] = block
        else:
            down = right(k * rows - half, rows)
            b[down, left(0, half)] = block
            b[down, right(0, half)] = a[here, half:]
    for k in range(4):
        here = slice(k * rows, (k + 1) * rows)
        if k < 2:
            block, across = turned[:, here], left(k * rows, rows)
        else:
            block, across = a[:half, here], right(k * rows - half, rows)
        b[left(0, half), across] = jnp.dot(hot, block, preferred_element_type=F32).astype(BF16)


def ready_kernel(onehot, force, mass_in, sums_in, force_m, weight_m, sums, mass, sem):
    copy = pltpu.make_async_copy(mass_in, mass, sem)
    copy.start()
    sums[...] = sums_in[...]
    half = onehot.shape[0]
    copy.wait()
    weight = 6.0 * column(mass[...])
    lane = lax.broadcasted_iota(jnp.int32, (half, 128), 1)
    three = triple(weight[:half])
    packed = jnp.where(
        lane == 0, three[:, :128].astype(F32), jnp.where(lane == 1, three[:, 128:256].astype(F32), three[:, 256:].astype(F32))
    )
    both = jnp.concatenate([triple(force[:half]), jnp.where(lane < 3, packed, 0.0).astype(BF16)], axis=1)
    moved = jnp.dot(onehot[...], both, preferred_element_type=F32)
    force_m[:half], force_m[half:] = by_pairs(fold(moved[:, :384]), force[half:])
    left = jnp.broadcast_to(jnp.sum(moved[:, 384:], axis=1, keepdims=True), (half, 128))
    weight_m[:half], weight_m[half:] = by_pairs(left, weight[half:])


def jump(f_a, f_b, from_a, from_b):
    sub = lax.axis_index("sub")
    alone = jnp.logical_or(sub == 0, sub == lax.axis_size("sub") - 1)
    return jnp.where(alone, 0.0, f_a[...] - from_a[...]), f_b[...] - from_b[...]


def part_kernel(b, f_b, from_b, part):
    half = f_b.shape[0]
    part[...] = jnp.dot(b[:, half:], pair(f_b[...] - from_b[...]), preferred_element_type=F32)


def first_kernel(b, part, y_a, y_b, from_a, from_b, order, q_a, q_b, t_a, t_b, sums):
    half = y_a.shape[0]
    r_a, r_b = jump(y_a, y_b, from_a, from_b)
    wide = part[...] + jnp.dot(b[:, :half], pair(r_a), preferred_element_type=F32)
    q = wide[:, :128]
    t = q + wide[:, 128:]
    q_a[...], q_b[...] = q[:half], q[half:]
    t_a[...], t_b[...] = t[:half], t[half:]
    rr = 0.5 * (add_up(r_a * r_a) + add_up(r_b * r_b))
    pw = add_up(r_a * q[:half]) + add_up(r_b * q[half:])
    sums[...] = jnp.concatenate([rr, pw, order[2:]], axis=0)


def second_kernel(b, part, q_a, q_b, from_a, from_b, sums, s_a, s_b, spread):
    half = q_a.shape[0]
    w_a, w_b = jump(q_a, q_b, from_a, from_b)
    wide = part[...] + jnp.dot(b[:, :half], pair(w_a), preferred_element_type=F32)
    s = wide[:, :128] + wide[:, 128:]
    s_a[...], s_b[...] = s[:half], s[half:]
    ww = 0.5 * (add_up(w_a * w_a) + add_up(w_b * w_b))
    wfw = add_up(w_a * s[:half]) + add_up(w_b * s[half:])
    own = jnp.concatenate([sums[:2], ww, wfw], axis=0)
    spread[...] = jnp.broadcast_to(own[None], spread.shape)


def corrected(gathered, y_a, y_b, q_a, q_b, t_a, t_b, s_a, s_b):
    total = jnp.sum(gathered[...], axis=0)
    rr, pw, ww, wfw = total[0:1], total[1:2], total[2:3], total[3:4]
    alpha = rr / pw
    ratio = ww / pw
    later = (alpha * alpha * ww - rr) / (alpha * alpha * (wfw - ww * ratio))
    gain = alpha * later

    def face(y, q, t, s):
        return y[...] - alpha * q[...] - gain * (ratio * t[...] - s[...])

    return face(y_a, q_a, t_a, s_a), face(y_b, q_b, t_b, s_b)


def next_kernel(b, gathered, y_a, y_b, q_a, q_b, t_a, t_b, s_a, s_b, force_m, weight_m, z_a, z_b, u_a, u_b):
    half = y_a.shape[0]
    new_a, new_b = corrected(gathered, y_a, y_b, q_a, q_b, t_a, t_b, s_a, s_b)
    u_a[...], u_b[...] = new_a, new_b
    rhs = (force_m[...] + weight_m[...] * jnp.concatenate([new_a, new_b], axis=0)).astype(BF16)
    y = jnp.dot(b[...], rhs, preferred_element_type=F32)
    z_a[...], z_b[...] = y[:half], y[half:]


def coarse(rate):
    scale = 1.0 / (1.0 + rate)
    return (1.0 - rate) * scale, 2.0 * scale, -2.0 * rate * scale


def early_kernel(onehot, u_a, u_b, base, rate_in, u_in, v_in, early_own, early_give, rate_own, order, rate, u, v, sem):
    copies = [
        pltpu.make_async_copy(source, target, sem.at[k]) for k, (source, target) in enumerate([(rate_in, rate), (u_in, u), (v_in, v)])
    ]
    for copy in copies:
        copy.start()
    order[...] = jnp.zeros(order.shape, F32)
    half = u_a.shape[0]
    left, right = by_sides(u_a[...], u_b[...])
    later = jnp.concatenate([to_left(onehot[...], left), right], axis=0)
    for copy in copies:
        copy.wait()
    tm = lax.axis_index("tm")
    rates = column(rate[...])
    even = lax.rem(tm, 2) == 0
    rate_own[...] = jnp.where(even, rates[:half], rates[half:])
    same, up, down = coarse(rates)
    early_u = -jnp.where(tm == 0, 0.0, same * u[...] + up * v[...])
    early_v = base[...] - 4.0 * later - jnp.where(tm == 0, 0.0, down * u[...] + same * v[...])
    for k, value in enumerate([early_u, early_v]):
        early_own[k] = jnp.where(even, value[:half], value[half:])
        early_give[k] = jnp.where(even, value[half:], value[:half])


def finish_kernel(onehot, gathered, y_a, y_b, q_a, q_b, t_a, t_b, s_a, s_b, face, give):
    odd = lax.rem(lax.axis_index("tm"), 2)
    left, right = by_sides(*corrected(gathered, y_a, y_b, q_a, q_b, t_a, t_b, s_a, s_b))

    @pl.when(odd == 0)
    def _():
        face[...] = left
        give[...] = right

    @pl.when(odd == 1)
    def _():
        face[...] = right
        give[...] = to_left(onehot[...], left)


def own_kernel(onehot, face, own):
    odd = lax.rem(lax.axis_index("tm"), 2)

    @pl.when(odd == 0)
    def _():
        own[...] = to_left(onehot[...], face[...])

    @pl.when(odd == 1)
    def _():
        own[...] = face[...]


def step_on(rate, state_u, state_v):
    same, up, down = coarse(rate)
    return same * state_u + up * state_v, down * state_u + same * state_v


def both_slices(own, got, early_own, early_got):
    even = lax.axis_index("tm") % 2 == 0
    mine = [own[...] + early_own[0], 2.0 * own[...] + early_own[1]]
    other = [got[...] + early_got[0], 2.0 * got[...] + early_got[1]]
    first = [jnp.where(even, mine[k], other[k]) for k in range(2)]
    return first, [jnp.where(even, other[k], mine[k]) for k in range(2)]


def combine_kernel(own, got, early_own, early_got, rate_own, blocks):
    rows = blocks.shape[2]
    first, second = both_slices(own, got, early_own, early_got)
    moved = step_on(rate_own[...], *first)
    for k in range(2):
        both = second[k] + moved[k]
        for place in range(blocks.shape[0]):
            blocks[place, k] = both[place * rows : (place + 1) * rows]


def prefix_kernel(blocks, rate_own, states):
    rows = blocks.shape[2]
    chip = lax.axis_index("tm") // 2
    rate = rate_own[pl.ds(pl.multiple_of(chip * rows, rows), rows)]
    states[0] = jnp.zeros(states.shape[1:], F32)
    state = [blocks[0, k] for k in range(2)]
    for place in range(1, blocks.shape[0]):
        for k in range(2):
            states[place, k] = state[k]
        if place + 1 < blocks.shape[0]:
            moved = step_on(rate, *step_on(rate, *state))
            state = [blocks[place, k] + moved[k] for k in range(2)]


def end_kernel(states, own, got, early_own, early_got, rate_own, stay, give):
    even = lax.axis_index("tm") % 2 == 0
    first, second = both_slices(own, got, early_own, early_got)
    rate = rate_own[...]
    entering = [jnp.concatenate([states[place, k] for place in range(states.shape[0])], axis=0) for k in range(2)]
    moved = step_on(rate, *entering)
    first = [first[k] + moved[k] for k in range(2)]
    moved = step_on(rate, *first)
    second = [second[k] + moved[k] for k in range(2)]
    for k in range(2):
        stay[k] = jnp.where(even, first[k], second[k])
        give[k] = jnp.where(even, second[k], first[k])


def copy_half(source, outs, start, sem):
    half = source.shape[1]
    place = pl.ds(pl.multiple_of(start, half), half)
    copies = [pltpu.make_async_copy(source.at[k], out.at[place], sem.at[k]) for k, out in enumerate(outs)]
    for copy in copies:
        copy.start()
    for copy in copies:
        copy.wait()


def keep_kernel(stay, end_u, end_v, sem):
    core = lax.rem(lax.axis_index("tm"), 2)
    copy_half(stay, [end_u, end_v], core * stay.shape[1], sem)


def join_kernel(got, in_u, in_v, end_u, end_v, sem):
    core = lax.rem(lax.axis_index("tm"), 2)
    copy_half(got, [end_u, end_v], (1 - core) * got.shape[1], sem)


def on_device(flex, mass, coarse_rate, face_perm, start_u, start_v, load):
    size, cases = start_u.shape[2:]
    half = size // 2
    subs, slices = lax.axis_size("sub"), lax.axis_size("tm")
    flex, mass, coarse_rate, face_perm, u, v, outer = [
        pltpu.with_memory_space_constraint(value, pltpu.HBM)
        for value in (flex[0], mass, coarse_rate, face_perm, start_u[0, 0], start_v[0, 0], load[0, 0])
    ]
    pairs = [[p for s in range(k, subs - 1, 2) for p in ((s, s + 1), (s + 1, s))] for k in (1, 0)]
    face = ((half, cases), F32)
    whole = ((size, cases), F32)
    wide = ((size, 2 * cases), F32)
    small = ((8, cases), F32)
    square = ((size, size), BF16)
    once = 2 * size * size * cases

    two = ((2, half, cases), F32)

    def swap(value):
        return lax.ppermute(value, "tm", [(t, t ^ 1) for t in range(slices)])

    def exchange(face_a, face_b):
        from_a = lax.ppermute(face_a, "sub", pairs[0])
        return from_a, lax.ppermute(face_b, "sub", pairs[1])

    a, onehot, y_a, y_b, base, force = call(
        start_kernel,
        "start",
        [square, ((half, half), BF16), face, face, whole, whole],
        (flex, u, v, outer, mass, face_perm),
        once,
        in_specs=[HBM] * 6,
        scratch=[
            pltpu.VMEM((size, cases), F32),
            pltpu.VMEM((size, cases), F32),
            pltpu.VMEM((size, cases), BF16),
            pltpu.VMEM((1, size), F32),
            pltpu.VMEM((1, half), jnp.int32),
            pltpu.SemaphoreType.DMA((5,)),
            pltpu.SemaphoreType.DMA((CHUNKS,)),
        ],
    )
    for step in range(2):
        from_a, from_b = exchange(y_a, y_b)
        if step == 0:
            matrix, order = call(
                prepare_kernel, "prepare", [square, small], (a, onehot), once, moved=half * cases, scratch=[pltpu.VMEM((half, half), BF16)]
            )
        else:
            early_own, early_give, rate_own, order = call(
                early_kernel,
                "early",
                [two, two, face, small],
                (onehot, u_a, u_b, base, coarse_rate, u, v),
                2 * half * half * 3 * cases,
                in_specs=[VMEM] * 4 + [HBM] * 3,
                scratch=[
                    pltpu.VMEM((1, size), F32),
                    pltpu.VMEM((size, cases), F32),
                    pltpu.VMEM((size, cases), F32),
                    pltpu.SemaphoreType.DMA((3,)),
                ],
            )
            early_got = swap(early_give)
        (part,) = call(part_kernel, "part", [wide], (matrix, y_b, from_b), once)
        q_a, q_b, t_a, t_b, sums = call(
            first_kernel, "first", [face] * 4 + [small], (matrix, part, y_a, y_b, from_a, from_b, order), once
        )
        from_a, from_b = exchange(q_a, q_b)
        if step == 0:
            force_m, weight_m, sums = call(
                ready_kernel,
                "ready",
                [whole, whole, small],
                (onehot, force, mass, sums),
                2 * half * half * 4 * cases,
                in_specs=[VMEM, VMEM, HBM, VMEM],
                scratch=[pltpu.VMEM((1, size), F32), pltpu.SemaphoreType.DMA(())],
            )
        (part,) = call(part_kernel, "part", [wide], (matrix, q_b, from_b), once)
        s_a, s_b, spread = call(
            second_kernel,
            "second",
            [face] * 2 + [((subs, 4, cases), F32)],
            (matrix, part, q_a, q_b, from_a, from_b, sums),
            once,
        )
        gathered = lax.all_to_all(spread, "sub", 0, 0, axis_index_groups=[list(range(subs))[::-1]])
        fields = (gathered, y_a, y_b, q_a, q_b, t_a, t_b, s_a, s_b)
        if step == 0:
            y_a, y_b, u_a, u_b = call(next_kernel, "next", [face] * 4, (matrix,) + fields + (force_m, weight_m), once)

    chips = slices // 2
    rows = half // chips
    blocks = ((chips, 2, rows, cases), F32)
    groups = [list(range(core, slices, 2)) for core in range(2)]
    light = size * cases * 10

    last, give = call(finish_kernel, "finish", [face, face], (onehot,) + fields, light)
    got = swap(give)
    (own,) = call(own_kernel, "own", [face], (onehot, last), light)
    halves = (own, got, early_own, early_got)
    (parts,) = call(combine_kernel, "combine", [blocks], halves + (rate_own,), light)
    parts = lax.all_to_all(parts, "tm", 0, 0, axis_index_groups=groups)
    (states,) = call(prefix_kernel, "prefix", [blocks], (parts, rate_own), light)
    states = lax.all_to_all(states, "tm", 0, 0, axis_index_groups=groups)
    stay, give = call(end_kernel, "end", [two, two], (states,) + halves + (rate_own,), light)
    got = swap(give)
    ends = dict(in_hbm=True, scratch=[pltpu.SemaphoreType.DMA((2,))])
    end_u, end_v = call(keep_kernel, "keep", [whole] * 2, (stay,), **ends)
    end_u, end_v = call(
        join_kernel, "join", [whole] * 2, (got, end_u, end_v), in_specs=[VMEM, HBM, HBM], aliases={1: 0, 2: 1}, **ends
    )
    return end_u[None, None], end_v[None, None]


def solution(mesh):
    return jax.shard_map(
        on_device,
        mesh=mesh,
        in_specs=(
            P("sub", None, None),
            P("sub", None),
            P("sub", None),
            P("sub", None),
            P("tm", "sub", None, None),
            P("tm", "sub", None, None),
            P("tm", "sub", None, None),
        ),
        out_specs=(P("tm", "sub", None, None), P("tm", "sub", None, None)),
        check_vma=False,
    )
```

```python
import jax
import jax.numpy as jnp
from jax import lax
from jax.experimental import pallas as pl
from jax.experimental.pallas import tpu as pltpu
from jax.sharding import PartitionSpec as P

F32 = jnp.float32
BF16 = jnp.bfloat16
VMEM = pl.BlockSpec(memory_space=pltpu.VMEM)
HBM = pl.BlockSpec(memory_space=pltpu.HBM)
CHUNKS = 8


def call(kernel, name, outs, args, flops=0, moved=None, in_specs=None, scratch=(), limit=12, in_hbm=False, aliases=None):
    moved = moved or sum(a.size * a.dtype.itemsize for a in args)
    return pl.pallas_call(
        kernel,
        name=name,
        out_shape=[(jax.ShapeDtypeStruct if in_hbm else pltpu.VMEM)(shape, dtype) for shape, dtype in outs],
        in_specs=in_specs or [VMEM] * len(args),
        out_specs=[HBM if in_hbm else VMEM] * len(outs),
        scratch_shapes=scratch,
        input_output_aliases=aliases or {},
        compiler_params=pltpu.CompilerParams(vmem_limit_bytes=limit * 2**20),
        cost_estimate=pl.CostEstimate(flops=flops, bytes_accessed=moved, transcendentals=0),
    )(*args)


def pair(value):
    high = value.astype(BF16)
    return jnp.concatenate([high, (value - high.astype(F32)).astype(BF16)], axis=1)


def triple(value):
    high = value.astype(BF16)
    rest = value - high.astype(F32)
    middle = rest.astype(BF16)
    low = (rest - middle.astype(F32)).astype(BF16)
    return jnp.concatenate([high, middle, low], axis=1)


def fold(wide):
    return wide[:, :128] + wide[:, 128:256] + wide[:, 256:]


def to_multipliers(onehot, face):
    return fold(jnp.dot(onehot, triple(face), preferred_element_type=F32))


def to_left(onehot, block):
    return fold(lax.dot_general(onehot, triple(block), (((0,), (0,)), ((), ())), preferred_element_type=F32))


def column(row):
    width = row.shape[1]
    pieces = [jnp.transpose(jnp.broadcast_to(row[:, k : k + 128], (128, 128))) for k in range(0, width, 128)]
    return jnp.concatenate(pieces, axis=0)


def add_up(value):
    return jnp.sum(value, axis=0, keepdims=True)


def is_even():
    return lax.rem(lax.axis_index("sub"), 2) == 0


def by_pairs(left, right):
    even = is_even()
    return jnp.where(even, left, right), jnp.where(even, right, left)


def by_sides(face_a, face_b):
    even = is_even()
    return jnp.where(even, face_a, face_b), jnp.where(even, face_b, face_a)


def sides(half, step):
    odd = lax.rem(lax.axis_index("sub"), 2)

    def left(offset, count):
        return pl.ds(pl.multiple_of(odd * half + offset, step), count)

    def right(offset, count):
        return pl.ds(pl.multiple_of((1 - odd) * half + offset, step), count)

    return left, right


def start_kernel(
    a_in, u_in, v_in, load_in, mass_in, perm_in, a, onehot, y_a, y_b, base, force, u, v, load, mass, perm, fields_sem, a_sem
):
    size = a.shape[0]
    half, rows = size // 2, size // CHUNKS
    small = [
        pltpu.make_async_copy(source, target, fields_sem.at[k])
        for k, (source, target) in enumerate(
            [(perm_in, perm), (mass_in, mass), (u_in, u), (v_in, v), (load_in, load)]
        )
    ]
    big = [
        pltpu.make_async_copy(a_in.at[pl.ds(k * rows, rows)], a.at[pl.ds(k * rows, rows)], a_sem.at[k])
        for k in range(CHUNKS)
    ]
    for copy in small + big[:2]:
        copy.start()
    small[0].wait()
    onehot[...] = (lax.broadcasted_iota(jnp.int32, (half, half), 0) == perm[...]).astype(F32).astype(BF16)
    for copy in small[1:]:
        copy.wait()
    for copy in big[2:]:
        copy.start()
    weight = 2.0 * column(mass[...])
    outer = load[...].astype(F32)
    rhs = (outer + weight * (u[...] + v[...])).astype(BF16)
    before = 2.0 * u[...] + v[...]
    base[...] = before
    force[...] = outer - weight * before
    faces = []
    for first in (0, CHUNKS // 2):
        parts = []
        for k in range(first, first + CHUNKS // 2):
            big[k].wait()
            parts.append(jnp.dot(a[k * rows : (k + 1) * rows], rhs, preferred_element_type=F32))
        faces.append(jnp.concatenate(parts, axis=0))
        if first == 0:
            faces[0] = to_multipliers(onehot[...], faces[0])
    y_a[...], y_b[...] = by_pairs(*faces)


def prepare_kernel(a, onehot, b, order, turned):
    order[...] = jnp.zeros(order.shape, F32)
    size = a.shape[0]
    half, rows = size // 2, size // 4
    left, right = sides(half, rows)
    hot = onehot[...]
    for k in range(4):
        here = slice(k * rows, (k + 1) * rows)
        block = lax.dot_general(a[here, :half], hot, (((1,), (1,)), ((), ())), preferred_element_type=F32).astype(BF16)
        if k < 2:
            turned[here] = block
        else:
            down = right(k * rows - half, rows)
            b[down, left(0, half)] = block
            b[down, right(0, half)] = a[here, half:]
    for k in range(4):
        here = slice(k * rows, (k + 1) * rows)
        if k < 2:
            block, across = turned[:, here], left(k * rows, rows)
        else:
            block, across = a[:half, here], right(k * rows - half, rows)
        b[left(0, half), across] = jnp.dot(hot, block, preferred_element_type=F32).astype(BF16)


def ready_kernel(onehot, force, mass_in, sums_in, force_m, weight_m, sums, mass, sem):
    copy = pltpu.make_async_copy(mass_in, mass, sem)
    copy.start()
    sums[...] = sums_in[...]
    half = onehot.shape[0]
    copy.wait()
    weight = 6.0 * column(mass[...])
    lane = lax.broadcasted_iota(jnp.int32, (half, 128), 1)
    three = triple(weight[:half])
    packed = jnp.where(
        lane == 0, three[:, :128].astype(F32), jnp.where(lane == 1, three[:, 128:256].astype(F32), three[:, 256:].astype(F32))
    )
    both = jnp.concatenate([triple(force[:half]), jnp.where(lane < 3, packed, 0.0).astype(BF16)], axis=1)
    moved = jnp.dot(onehot[...], both, preferred_element_type=F32)
    force_m[:half], force_m[half:] = by_pairs(fold(moved[:, :384]), force[half:])
    left = jnp.broadcast_to(jnp.sum(moved[:, 384:], axis=1, keepdims=True), (half, 128))
    weight_m[:half], weight_m[half:] = by_pairs(left, weight[half:])


def jump(f_a, f_b, from_a, from_b):
    sub = lax.axis_index("sub")
    alone = jnp.logical_or(sub == 0, sub == lax.axis_size("sub") - 1)
    return jnp.where(alone, 0.0, f_a[...] - from_a[...]), f_b[...] - from_b[...]


def part_kernel(b, f_b, from_b, part):
    half = f_b.shape[0]
    part[...] = jnp.dot(b[:, half:], pair(f_b[...] - from_b[...]), preferred_element_type=F32)


def first_kernel(b, part, y_a, y_b, from_a, from_b, order, q_a, q_b, t_a, t_b, sums):
    half = y_a.shape[0]
    r_a, r_b = jump(y_a, y_b, from_a, from_b)
    wide = part[...] + jnp.dot(b[:, :half], pair(r_a), preferred_element_type=F32)
    q = wide[:, :128]
    t = q + wide[:, 128:]
    q_a[...], q_b[...] = q[:half], q[half:]
    t_a[...], t_b[...] = t[:half], t[half:]
    rr = 0.5 * (add_up(r_a * r_a) + add_up(r_b * r_b))
    pw = add_up(r_a * q[:half]) + add_up(r_b * q[half:])
    sums[...] = jnp.concatenate([rr, pw, order[2:]], axis=0)


def second_kernel(b, part, q_a, q_b, from_a, from_b, sums, s_a, s_b, spread):
    half = q_a.shape[0]
    w_a, w_b = jump(q_a, q_b, from_a, from_b)
    wide = part[...] + jnp.dot(b[:, :half], pair(w_a), preferred_element_type=F32)
    s = wide[:, :128] + wide[:, 128:]
    s_a[...], s_b[...] = s[:half], s[half:]
    ww = 0.5 * (add_up(w_a * w_a) + add_up(w_b * w_b))
    wfw = add_up(w_a * s[:half]) + add_up(w_b * s[half:])
    own = jnp.concatenate([sums[:2], ww, wfw], axis=0)
    spread[...] = jnp.broadcast_to(own[None], spread.shape)


def corrected(gathered, y_a, y_b, q_a, q_b, t_a, t_b, s_a, s_b):
    total = jnp.sum(gathered[...], axis=0)
    rr, pw, ww, wfw = total[0:1], total[1:2], total[2:3], total[3:4]
    alpha = rr / pw
    ratio = ww / pw
    later = (alpha * alpha * ww - rr) / (alpha * alpha * (wfw - ww * ratio))
    gain = alpha * later

    def face(y, q, t, s):
        return y[...] - alpha * q[...] - gain * (ratio * t[...] - s[...])

    return face(y_a, q_a, t_a, s_a), face(y_b, q_b, t_b, s_b)


def next_kernel(b, gathered, y_a, y_b, q_a, q_b, t_a, t_b, s_a, s_b, force_m, weight_m, z_a, z_b, u_a, u_b):
    half = y_a.shape[0]
    new_a, new_b = corrected(gathered, y_a, y_b, q_a, q_b, t_a, t_b, s_a, s_b)
    u_a[...], u_b[...] = new_a, new_b
    rhs = (force_m[...] + weight_m[...] * jnp.concatenate([new_a, new_b], axis=0)).astype(BF16)
    y = jnp.dot(b[...], rhs, preferred_element_type=F32)
    z_a[...], z_b[...] = y[:half], y[half:]


def coarse(rate):
    scale = 1.0 / (1.0 + rate)
    return (1.0 - rate) * scale, 2.0 * scale, -2.0 * rate * scale


def early_kernel(onehot, u_a, u_b, base, rate_in, u_in, v_in, early_u, early_v, rate_own, order, rate, u, v, sem):
    copies = [
        pltpu.make_async_copy(source, target, sem.at[k]) for k, (source, target) in enumerate([(rate_in, rate), (u_in, u), (v_in, v)])
    ]
    for copy in copies:
        copy.start()
    order[...] = jnp.zeros(order.shape, F32)
    half = u_a.shape[0]
    left, right = by_sides(u_a[...], u_b[...])
    later = jnp.concatenate([to_left(onehot[...], left), right], axis=0)
    for copy in copies:
        copy.wait()
    tm = lax.axis_index("tm")
    rates = column(rate[...])
    rate_own[...] = jnp.where(tm % 2 == 0, rates[:half], rates[half:])
    same, up, down = coarse(rates)
    early_u[...] = -jnp.where(tm == 0, 0.0, same * u[...] + up * v[...])
    early_v[...] = base[...] - 4.0 * later - jnp.where(tm == 0, 0.0, down * u[...] + same * v[...])


def finish_kernel(onehot, gathered, y_a, y_b, q_a, q_b, t_a, t_b, s_a, s_b, early_u, early_v, face, give):
    odd = lax.rem(lax.axis_index("tm"), 2)
    half = y_a.shape[0]
    left, right = by_sides(*corrected(gathered, y_a, y_b, q_a, q_b, t_a, t_b, s_a, s_b))

    @pl.when(odd == 0)
    def _():
        face[...] = left
        give[0] = right + early_u[half:]
        give[1] = 2.0 * right + early_v[half:]

    @pl.when(odd == 1)
    def _():
        face[...] = right
        ordered = to_left(onehot[...], left)
        give[0] = ordered + early_u[:half]
        give[1] = 2.0 * ordered + early_v[:half]


def own_kernel(onehot, face, early_u, early_v, own):
    odd = lax.rem(lax.axis_index("tm"), 2)
    half = face.shape[0]

    @pl.when(odd == 0)
    def _():
        ordered = to_left(onehot[...], face[...])
        own[0] = ordered + early_u[:half]
        own[1] = 2.0 * ordered + early_v[:half]

    @pl.when(odd == 1)
    def _():
        own[0] = face[...] + early_u[half:]
        own[1] = 2.0 * face[...] + early_v[half:]


def step_on(rate, state_u, state_v):
    same, up, down = coarse(rate)
    return same * state_u + up * state_v, down * state_u + same * state_v


def both_slices(own, got):
    even = lax.axis_index("tm") % 2 == 0
    return [jnp.where(even, own[k], got[k]) for k in range(2)], [jnp.where(even, got[k], own[k]) for k in range(2)]


def combine_kernel(own, got, rate_own, blocks):
    rows = blocks.shape[2]
    first, second = both_slices(own, got)
    moved = step_on(rate_own[...], *first)
    for k in range(2):
        both = second[k] + moved[k]
        for place in range(blocks.shape[0]):
            blocks[place, k] = both[place * rows : (place + 1) * rows]


def prefix_kernel(blocks, rate_own, states):
    rows = blocks.shape[2]
    chip = lax.axis_index("tm") // 2
    rate = rate_own[pl.ds(pl.multiple_of(chip * rows, rows), rows)]
    states[0] = jnp.zeros(states.shape[1:], F32)
    state = [blocks[0, k] for k in range(2)]
    for place in range(1, blocks.shape[0]):
        for k in range(2):
            states[place, k] = state[k]
        if place + 1 < blocks.shape[0]:
            moved = step_on(rate, *step_on(rate, *state))
            state = [blocks[place, k] + moved[k] for k in range(2)]


def end_kernel(states, own, got, rate_own, stay, give):
    even = lax.axis_index("tm") % 2 == 0
    first, second = both_slices(own, got)
    rate = rate_own[...]
    entering = [jnp.concatenate([states[place, k] for place in range(states.shape[0])], axis=0) for k in range(2)]
    moved = step_on(rate, *entering)
    first = [first[k] + moved[k] for k in range(2)]
    moved = step_on(rate, *first)
    second = [second[k] + moved[k] for k in range(2)]
    for k in range(2):
        stay[k] = jnp.where(even, first[k], second[k])
        give[k] = jnp.where(even, second[k], first[k])


def copy_half(source, outs, start, sem):
    half = source.shape[1]
    place = pl.ds(pl.multiple_of(start, half), half)
    copies = [pltpu.make_async_copy(source.at[k], out.at[place], sem.at[k]) for k, out in enumerate(outs)]
    for copy in copies:
        copy.start()
    for copy in copies:
        copy.wait()


def keep_kernel(stay, end_u, end_v, sem):
    core = lax.rem(lax.axis_index("tm"), 2)
    copy_half(stay, [end_u, end_v], core * stay.shape[1], sem)


def join_kernel(got, in_u, in_v, end_u, end_v, sem):
    core = lax.rem(lax.axis_index("tm"), 2)
    copy_half(got, [end_u, end_v], (1 - core) * got.shape[1], sem)


def on_device(flex, mass, coarse_rate, face_perm, start_u, start_v, load):
    size, cases = start_u.shape[2:]
    half = size // 2
    subs, slices = lax.axis_size("sub"), lax.axis_size("tm")
    flex, mass, coarse_rate, face_perm, u, v, outer = [
        pltpu.with_memory_space_constraint(value, pltpu.HBM)
        for value in (flex[0], mass, coarse_rate, face_perm, start_u[0, 0], start_v[0, 0], load[0, 0])
    ]
    pairs = [[p for s in range(k, subs - 1, 2) for p in ((s, s + 1), (s + 1, s))] for k in (1, 0)]
    face = ((half, cases), F32)
    whole = ((size, cases), F32)
    wide = ((size, 2 * cases), F32)
    small = ((8, cases), F32)
    square = ((size, size), BF16)
    once = 2 * size * size * cases

    def exchange(face_a, face_b):
        from_a = lax.ppermute(face_a, "sub", pairs[0])
        return from_a, lax.ppermute(face_b, "sub", pairs[1])

    a, onehot, y_a, y_b, base, force = call(
        start_kernel,
        "start",
        [square, ((half, half), BF16), face, face, whole, whole],
        (flex, u, v, outer, mass, face_perm),
        once,
        in_specs=[HBM] * 6,
        scratch=[
            pltpu.VMEM((size, cases), F32),
            pltpu.VMEM((size, cases), F32),
            pltpu.VMEM((size, cases), BF16),
            pltpu.VMEM((1, size), F32),
            pltpu.VMEM((1, half), jnp.int32),
            pltpu.SemaphoreType.DMA((5,)),
            pltpu.SemaphoreType.DMA((CHUNKS,)),
        ],
    )
    for step in range(2):
        from_a, from_b = exchange(y_a, y_b)
        if step == 0:
            matrix, order = call(
                prepare_kernel, "prepare", [square, small], (a, onehot), once, moved=half * cases, scratch=[pltpu.VMEM((half, half), BF16)]
            )
        else:
            early_u, early_v, rate_own, order = call(
                early_kernel,
                "early",
                [whole, whole, face, small],
                (onehot, u_a, u_b, base, coarse_rate, u, v),
                2 * half * half * 3 * cases,
                in_specs=[VMEM] * 4 + [HBM] * 3,
                scratch=[
                    pltpu.VMEM((1, size), F32),
                    pltpu.VMEM((size, cases), F32),
                    pltpu.VMEM((size, cases), F32),
                    pltpu.SemaphoreType.DMA((3,)),
                ],
            )
        (part,) = call(part_kernel, "part", [wide], (matrix, y_b, from_b), once)
        q_a, q_b, t_a, t_b, sums = call(
            first_kernel, "first", [face] * 4 + [small], (matrix, part, y_a, y_b, from_a, from_b, order), once
        )
        from_a, from_b = exchange(q_a, q_b)
        if step == 0:
            force_m, weight_m, sums = call(
                ready_kernel,
                "ready",
                [whole, whole, small],
                (onehot, force, mass, sums),
                2 * half * half * 4 * cases,
                in_specs=[VMEM, VMEM, HBM, VMEM],
                scratch=[pltpu.VMEM((1, size), F32), pltpu.SemaphoreType.DMA(())],
            )
        (part,) = call(part_kernel, "part", [wide], (matrix, q_b, from_b), once)
        s_a, s_b, spread = call(
            second_kernel,
            "second",
            [face] * 2 + [((subs, 4, cases), F32)],
            (matrix, part, q_a, q_b, from_a, from_b, sums),
            once,
        )
        gathered = lax.all_to_all(spread, "sub", 0, 0, axis_index_groups=[list(range(subs))[::-1]])
        fields = (gathered, y_a, y_b, q_a, q_b, t_a, t_b, s_a, s_b)
        if step == 0:
            y_a, y_b, u_a, u_b = call(next_kernel, "next", [face] * 4, (matrix,) + fields + (force_m, weight_m), once)

    chips = slices // 2
    rows = half // chips
    two = ((2, half, cases), F32)
    blocks = ((chips, 2, rows, cases), F32)
    groups = [list(range(core, slices, 2)) for core in range(2)]
    light = size * cases * 10

    def swap(value):
        return lax.ppermute(value, "tm", [(t, t ^ 1) for t in range(slices)])

    last, give = call(finish_kernel, "finish", [face, two], (onehot,) + fields + (early_u, early_v), light)
    got = swap(give)
    (own,) = call(own_kernel, "own", [two], (onehot, last, early_u, early_v), light)
    (parts,) = call(combine_kernel, "combine", [blocks], (own, got, rate_own), light)
    parts = lax.all_to_all(parts, "tm", 0, 0, axis_index_groups=groups)
    (states,) = call(prefix_kernel, "prefix", [blocks], (parts, rate_own), light)
    states = lax.all_to_all(states, "tm", 0, 0, axis_index_groups=groups)
    stay, give = call(end_kernel, "end", [two, two], (states, own, got, rate_own), light)
    got = swap(give)
    ends = dict(in_hbm=True, scratch=[pltpu.SemaphoreType.DMA((2,))])
    end_u, end_v = call(keep_kernel, "keep", [whole] * 2, (stay,), **ends)
    end_u, end_v = call(
        join_kernel, "join", [whole] * 2, (got, end_u, end_v), in_specs=[VMEM, HBM, HBM], aliases={1: 0, 2: 1}, **ends
    )
    return end_u[None, None], end_v[None, None]


def solution(mesh):
    return jax.shard_map(
        on_device,
        mesh=mesh,
        in_specs=(
            P("sub", None, None),
            P("sub", None),
            P("sub", None),
            P("sub", None),
            P("tm", "sub", None, None),
            P("tm", "sub", None, None),
            P("tm", "sub", None, None),
        ),
        out_specs=(P("tm", "sub", None, None), P("tm", "sub", None, None)),
        check_vma=False,
    )
```
